32 devices in a mesh: grp: 4 (over y, x), sp: 8 (over z, core).
Axes of the slice: x: 2, y: 2, z: 4, core: 2. Of those that a mesh axis runs over, the one named last changes fastest.
Arguments:
- queries: bfloat16 [4, 512, 1024], P('grp', 'sp'), may hold values from -180 to 180
- keys: bfloat16 [4, 512, 1024], P('grp', 'sp'), may hold values from -7 to 7
- values: bfloat16 [4, 512, 1024], P('grp', 'sp'), may hold values from -6 to 6
- positions: int32 [4, 512], P('grp'), may hold values from 0 to 511, each once within a row
- anchor: int32 [1], replicated, may hold values from 0 to 262143
Outputs:
- attended: bfloat16 [4, 512, 1024], P('grp', 'sp')
The draws below stay inside these ranges and needn't reach their ends.
Inputs may be any that keep to these rules, and one draw needn't show every extreme that they name: Each group's row of positions holds every number of 0 to 511 once.
All inputs are finite; a program needn't handle non-finite values.
Results may differ from the reference program's by a relative error of at most 0.0048.
Values may be sent and summed in bfloat16 or wider, within the bound.
No kernel may reach another device: no remote copies, remote signals or barrier semaphores. Data moves between devices by JAX's collectives and lax.ppermute only.
A program may use at most 64 MiB of HBM per device.

```python
import math
import jax
import jax.numpy as jnp
from jax import lax

HD = 128
HEADS = 8
D = 1024
LEN = 512
GROUPS = 4


def draw_keys(key, part):
    noise = jnp.clip(jax.random.normal(jax.random.fold_in(key, 12), (GROUPS, LEN, D), jnp.float32), -6.0, 6.0)
    result = noise
    return result.astype(jnp.bfloat16)


def draw_queries(key, part):
    noise = jnp.clip(jax.random.normal(jax.random.fold_in(key, 13), (GROUPS, LEN, D), jnp.float32), -6.0, 6.0)
    result = noise
    return result.astype(jnp.bfloat16)


def level_of(own_key, extent, pieces, least, largest):
    gain, own = 1.0, jax.random.fold_in(own_key, 6)
    for axis_at, parts in pieces:
        draws = jnp.exp(jax.random.uniform(jax.random.fold_in(own, axis_at), (parts,), jnp.float32, least / len(pieces), largest / len(pieces)))
        gain = gain * jnp.repeat(draws, extent[axis_at] // parts).reshape([-1 if axis == axis_at else 1 for axis in range(len(extent))])
    return gain


def centred(rng, shape, spread, bound, split=(), kind=jnp.bfloat16):
    loudness = level_of(rng, shape, split, -0.22, 0.18) if split else 1.0
    values = jax.random.normal(rng, shape, jnp.float32) * spread * loudness
    return jnp.minimum(jnp.maximum(values, -bound), bound).astype(kind)


def setup_inputs(seed: int = 0) -> dict:
    key_list = jax.random.split(jax.random.key(seed), 6)
    queries = draw_queries(jax.random.fold_in(key_list[5], 71), 0)
    keys = draw_keys(jax.random.fold_in(key_list[5], 71), 0)
    values = centred(key_list[2], (GROUPS, LEN, D), 1.0, 6.0, ((0, 4), (1, 8)))
    positions = jax.vmap(lambda own: jax.random.permutation(own, LEN))(jax.random.split(key_list[3], GROUPS)).reshape((GROUPS, LEN)).astype(jnp.int32)
    anchor = jax.random.randint(key_list[4], (1,), 0, GROUPS * 65536).astype(jnp.int32)
    return {"queries": queries, "keys": keys, "values": values, "positions": positions, "anchor": anchor}


NEG = -1e+30

def reference(queries, keys, values, positions, anchor):
    anchor_index = (anchor[0] % GROUPS).astype(jnp.int32)
    anchor_keys = keys[anchor_index]
    anchor_values = values[anchor_index]
    score_scale = 1.0 / math.sqrt(HD)

    def one_group(group_index):
        q_rows = queries[group_index]
        k_rows = keys[group_index]
        v_rows = values[group_index]
        order = positions[group_index]
        visible = order[None, :] <= order[:, None]
        skip_anchor = group_index == anchor_index

        def one_head(head_index):
            start = head_index * HD
            q_head = lax.dynamic_slice_in_dim(q_rows, start, HD, 1)
            k_head = lax.dynamic_slice_in_dim(k_rows, start, HD, 1)
            v_head = lax.dynamic_slice_in_dim(v_rows, start, HD, 1)
            ak_head = lax.dynamic_slice_in_dim(anchor_keys, start, HD, 1)
            av_head = lax.dynamic_slice_in_dim(anchor_values, start, HD, 1)
            local_scores = jnp.dot(q_head, k_head.T, preferred_element_type=jnp.float32) * score_scale
            far_scores = jnp.dot(q_head, ak_head.T, preferred_element_type=jnp.float32) * score_scale
            local_scores = jnp.where(visible, local_scores, NEG)
            far_scores = jnp.where(skip_anchor, NEG, far_scores)
            joined = jnp.concatenate([local_scores, far_scores], 1)
            top_score = lax.optimization_barrier(jnp.max(joined, axis=1, keepdims=True))
            expo = jnp.exp(joined - top_score)
            probs = (expo / lax.optimization_barrier(jnp.sum(expo, axis=1, keepdims=True))).astype(jnp.bfloat16)
            value_rows = jnp.concatenate([v_head, av_head], 0)
            return jnp.dot(probs, value_rows, preferred_element_type=jnp.float32).astype(jnp.bfloat16)
        per_head = lax.map(one_head, jnp.arange(HEADS, dtype=jnp.int32))
        return jnp.transpose(per_head, (1, 0, 2)).reshape(LEN, D)
    return lax.map(one_group, jnp.arange(GROUPS, dtype=jnp.int32))
```

```python
import math

import jax
import jax.numpy as jnp
from jax import lax
from jax.experimental import pallas as pl
from jax.experimental.pallas import tpu as pltpu
from jax.sharding import PartitionSpec as P

HD = 128
CORES = 2
NEG = -1e30
VMEM_LIMIT = 48 * 2**20


def in_vmem(count):
    return [pl.BlockSpec(memory_space=pltpu.VMEM)] * count


def resident(x):
    return pltpu.with_memory_space_constraint(x, pltpu.VMEM)


def swap(x, axis, flip):
    return lax.ppermute(x, axis, [(i, i ^ flip) for i in range(lax.axis_size(axis))])


def pack(queries, keys, values, chips):
    rows, width = queries.shape[1], queries.shape[2] // chips

    def body(q_ref, k_ref, v_ref, *rest):
        kv_refs, q_refs, sems = rest[:chips], rest[chips : 2 * chips], rest[-1]
        chip = lax.axis_index("sp") // CORES
        copies = []
        for flip in range(chips):
            columns = pl.ds(pl.multiple_of((chip ^ flip) * width, HD), width)
            for source, target in (
                (k_ref.at[0, :, columns], kv_refs[flip].at[0]),
                (v_ref.at[0, :, columns], kv_refs[flip].at[1]),
                (q_ref.at[0, :, columns], q_refs[flip]),
            ):
                copies.append(pltpu.make_async_copy(source, target, sems.at[len(copies)]))
        for copy in copies:
            copy.start()
        for copy in copies:
            copy.wait()

    outs = pl.pallas_call(
        body,
        out_shape=[pltpu.VMEM((2, rows, width), keys.dtype)] * chips
        + [pltpu.VMEM((rows, width), queries.dtype)] * chips,
        in_specs=[pl.BlockSpec(memory_space=pl.ANY)] * 3,
        out_specs=in_vmem(2 * chips),
        scratch_shapes=[pltpu.SemaphoreType.DMA((3 * chips,))],
        name="pack",
    )(queries, keys, values)
    return outs[:chips], outs[chips:]


def join(blocks):
    chips = len(blocks)
    _, rows, width = blocks[0].shape

    def body(*refs):
        block_refs, (k_ref, v_ref) = refs[:chips], refs[chips:]
        chip = lax.axis_index("sp") // CORES
        for flip, block in enumerate(block_refs):
            place = pl.ds(pl.multiple_of((chip ^ flip) * rows, rows), rows)
            k_ref[place, :] = block[0]
            v_ref[place, :] = block[1]

    return pl.pallas_call(
        body,
        out_shape=[pltpu.VMEM((chips * rows, width), blocks[0].dtype)] * 2,
        in_specs=in_vmem(chips),
        out_specs=in_vmem(2),
        name="join",
    )(*[resident(b) for b in blocks])


def scores_of(q, k_ref, columns):
    return lax.dot_general(
        q, k_ref[:, columns], (((1,), (1,)), ((), ())), preferred_element_type=jnp.float32
    )


def near(q_blocks, k_own, v_own, k_other, v_other, places):
    chips = len(q_blocks)
    rows, width = q_blocks[0].shape
    heads, length = width // HD, chips * rows
    step = min(256, length)
    scale = 1.0 / (math.sqrt(HD) * math.log(2.0))

    def body(*refs):
        q_refs = refs[:chips]
        ko, vo, kt, vt, at, q_all, top_ref, sum_ref, acc_ref = refs[chips:]
        chip, core = lax.axis_index("sp") // CORES, lax.axis_index("sp") % CORES
        for flip, block in enumerate(q_refs):
            q_all[pl.ds(pl.multiple_of((chip ^ flip) * rows, rows), rows), :] = block[...]
        own = at[pl.ds(core, 1), :]
        other = at[pl.ds(1 - core, 1), :]

        def chunk(index):
            start = pl.multiple_of(index * step, step)
            here = pl.ds(start, step)
            row = own if step == length else at[pl.ds(core, 1), here]
            order = jnp.transpose(jnp.broadcast_to(row, (HD, step)))[:, :1]
            for head in range(heads):
                columns = slice(head * HD, (head + 1) * HD)
                q = q_all[here, columns]
                first = jnp.where(own <= order, scores_of(q, ko, columns), NEG)
                second = jnp.where(other <= order, scores_of(q, kt, columns), NEG)
                top = jnp.maximum(
                    jnp.max(first, axis=1, keepdims=True), jnp.max(second, axis=1, keepdims=True)
                )
                first = jnp.exp2((first - top) * scale)
                second = jnp.exp2((second - top) * scale)
                total = jnp.sum(first, axis=1, keepdims=True) + jnp.sum(second, axis=1, keepdims=True)
                acc = jnp.dot(
                    first.astype(jnp.bfloat16), vo[:, columns], preferred_element_type=jnp.float32
                ) + jnp.dot(
                    second.astype(jnp.bfloat16), vt[:, columns], preferred_element_type=jnp.float32
                )
                top_ref[head, here, :] = jnp.broadcast_to(top, (step, HD))
                sum_ref[head, here, :] = jnp.broadcast_to(total, (step, HD))
                acc_ref[here, columns] = acc

        if length == step:
            chunk(0)
        else:
            pl.loop(0, length // step)(chunk)

    state = pltpu.VMEM((heads, length, HD), jnp.float32)
    return pl.pallas_call(
        body,
        out_shape=[
            pltpu.VMEM((length, width), q_blocks[0].dtype),
            state,
            state,
            pltpu.VMEM((length, width), jnp.float32),
        ],
        in_specs=in_vmem(chips + 5),
        out_specs=in_vmem(4),
        compiler_params=pltpu.CompilerParams(vmem_limit_bytes=VMEM_LIMIT),
        cost_estimate=pl.CostEstimate(
            flops=8 * length * length * width, bytes_accessed=0, transcendentals=2 * length * length * heads
        ),
        name="near",
    )(*[resident(x) for x in (*q_blocks, k_own, v_own, k_other, v_other)], places)


def far(q_all, top_in, sum_in, acc_in, k_own, v_own, k_other, v_other, skip, chips):
    length, width = q_all.shape
    rows, heads = length // chips, width // HD
    step = min(256, length)
    scale = 1.0 / (math.sqrt(HD) * math.log(2.0))

    def body(skip_ref, q_ref, top_ref, sum_ref, acc_ref, ko, vo, kt, vt, *rest):
        out_refs, done = rest[:chips], rest[chips]
        chip = lax.axis_index("sp") // CORES
        hidden = skip_ref[0] != 0

        def chunk(index):
            here = pl.ds(pl.multiple_of(index * step, step), step)
            for head in range(heads):
                columns = slice(head * HD, (head + 1) * HD)
                q = q_ref[here, columns]
                first = jnp.where(hidden, NEG, scores_of(q, ko, columns))
                second = jnp.where(hidden, NEG, scores_of(q, kt, columns))
                old = top_ref[head, here, :][:, :1]
                top = jnp.maximum(
                    old,
                    jnp.maximum(
                        jnp.max(first, axis=1, keepdims=True), jnp.max(second, axis=1, keepdims=True)
                    ),
                )
                keep = jnp.exp2((old - top) * scale)
                first = jnp.exp2((first - top) * scale)
                second = jnp.exp2((second - top) * scale)
                total = (
                    keep * sum_ref[head, here, :][:, :1]
                    + jnp.sum(first, axis=1, keepdims=True)
                    + jnp.sum(second, axis=1, keepdims=True)
                )
                acc = (
                    keep * acc_ref[here, columns]
                    + jnp.dot(first.astype(jnp.bfloat16), vo[:, columns], preferred_element_type=jnp.float32)
                    + jnp.dot(second.astype(jnp.bfloat16), vt[:, columns], preferred_element_type=jnp.float32)
                )
                done[here, columns] = (acc / total).astype(jnp.bfloat16)

        if length == step:
            chunk(0)
        else:
            pl.loop(0, length // step)(chunk)
        for flip, out in enumerate(out_refs):
            out[...] = done[pl.ds(pl.multiple_of((chip ^ flip) * rows, rows), rows), :]

    return pl.pallas_call(
        body,
        out_shape=[pltpu.VMEM((rows, width), jnp.bfloat16)] * chips,
        in_specs=[pl.BlockSpec(memory_space=pltpu.SMEM)] + in_vmem(8),
        out_specs=in_vmem(chips),
        scratch_shapes=[pltpu.VMEM((length, width), jnp.bfloat16)],
        compiler_params=pltpu.CompilerParams(vmem_limit_bytes=VMEM_LIMIT),
        cost_estimate=pl.CostEstimate(
            flops=8 * length * length * width, bytes_accessed=0, transcendentals=2 * length * length * heads
        ),
        name="far",
    )(skip, *[resident(x) for x in (q_all, top_in, sum_in, acc_in, k_own, v_own, k_other, v_other)])


def unpack(blocks):
    chips = len(blocks)
    rows, width = blocks[0].shape

    def body(*refs):
        block_refs, out_ref, sems = refs[:chips], refs[chips], refs[-1]
        chip = lax.axis_index("sp") // CORES
        copies = []
        for flip, block in enumerate(block_refs):
            columns = pl.ds(pl.multiple_of((chip ^ flip) * width, HD), width)
            copies.append(pltpu.make_async_copy(block, out_ref.at[0, :, columns], sems.at[flip]))
        for copy in copies:
            copy.start()
        for copy in copies:
            copy.wait()

    return pl.pallas_call(
        body,
        out_shape=jax.ShapeDtypeStruct((1, rows, chips * width), blocks[0].dtype),
        in_specs=in_vmem(chips),
        out_specs=pl.BlockSpec(memory_space=pl.ANY),
        scratch_shapes=[pltpu.SemaphoreType.DMA((chips,))],
        name="unpack",
    )(*[resident(b) for b in blocks])


def on_device(queries, keys, values, positions, anchor):
    groups, chips = lax.axis_size("grp"), lax.axis_size("sp") // CORES
    bits = groups.bit_length() - 1
    root, group = anchor[0] % groups, lax.axis_index("grp")
    rows = queries.shape[1]

    kv_blocks, q_blocks = pack(queries, keys, values, chips)
    kv_all = [kv_blocks[0]] + [swap(kv_blocks[f], "sp", CORES * f) for f in range(1, chips)]
    q_all = [q_blocks[0]] + [swap(q_blocks[f], "sp", CORES * f) for f in range(1, chips)]
    k_own, v_own = join(kv_all)

    k_far, v_far = k_own, v_own
    for stage in range(bits):
        for which in range(2):
            bit = stage if which == 0 else bits - 1 - stage
            mine = ((root >> bit) & 1) == ((group >> bit) & 1)
            if which == 0:
                k_far = jnp.where(mine, k_far, swap(k_far, "grp", 1 << bit))
            else:
                v_far = jnp.where(mine, v_far, swap(v_far, "grp", 1 << bit))
    k_other, v_other = swap(k_own, "sp", 1), swap(v_own, "sp", 1)
    k_far_other, v_far_other = swap(k_far, "sp", 1), swap(v_far, "sp", 1)

    places = jnp.swapaxes(positions.reshape(chips, CORES, rows), 0, 1).reshape(CORES, chips * rows)
    q_rows, top, total, acc = near(q_all, k_own, v_own, k_other, v_other, places)
    skip = (group == root).astype(jnp.int32).reshape(1)
    done = far(q_rows, top, total, acc, k_far, v_far, k_far_other, v_far_other, skip, chips)
    back = [done[0]] + [swap(done[f], "sp", CORES * f) for f in range(1, chips)]
    return unpack(back)


def solution(mesh):
    return jax.shard_map(
        on_device,
        mesh=mesh,
        in_specs=(
            P("grp", "sp", None),
            P("grp", "sp", None),
            P("grp", "sp", None),
            P("grp", None),
            P(),
        ),
        out_specs=P("grp", "sp", None),
        check_vma=False,
    )
```

```python
import math

import jax
import jax.numpy as jnp
from jax import lax
from jax.experimental import pallas as pl
from jax.experimental.pallas import tpu as pltpu
from jax.sharding import PartitionSpec as P

HD = 128
CORES = 2
NEG = -1e30
VMEM_LIMIT = 48 * 2**20


def in_vmem(count):
    return [pl.BlockSpec(memory_space=pltpu.VMEM)] * count


def resident(x):
    return pltpu.with_memory_space_constraint(x, pltpu.VMEM)


def swap(x, axis, flip):
    return lax.ppermute(x, axis, [(i, i ^ flip) for i in range(lax.axis_size(axis))])


def pack(queries, keys, values, chips):
    rows, width = queries.shape[1], queries.shape[2] // chips

    def body(q_ref, k_ref, v_ref, *rest):
        block_refs, sems = rest[:chips], rest[-1]
        chip = lax.axis_index("sp") // CORES
        copies = []
        for flip in range(chips):
            columns = pl.ds(pl.multiple_of((chip ^ flip) * width, HD), width)
            for part, source in enumerate((q_ref, k_ref, v_ref)):
                copies.append(
                    pltpu.make_async_copy(
                        source.at[0, :, columns], block_refs[flip].at[part], sems.at[len(copies)]
                    )
                )
        for copy in copies:
            copy.start()
        for copy in copies:
            copy.wait()

    return pl.pallas_call(
        body,
        out_shape=[pltpu.VMEM((3, rows, width), keys.dtype)] * chips,
        in_specs=[pl.BlockSpec(memory_space=pl.ANY)] * 3,
        out_specs=in_vmem(chips),
        scratch_shapes=[pltpu.SemaphoreType.DMA((3 * chips,))],
        name="pack",
    )(queries, keys, values)


def join(blocks):
    chips = len(blocks)
    _, rows, width = blocks[0].shape

    def body(*refs):
        block_refs, out_refs = refs[:chips], refs[chips:]
        chip = lax.axis_index("sp") // CORES
        for flip, block in enumerate(block_refs):
            place = pl.ds(pl.multiple_of((chip ^ flip) * rows, rows), rows)
            for part, out in enumerate(out_refs):
                out[place, :] = block[part]

    return pl.pallas_call(
        body,
        out_shape=[pltpu.VMEM((chips * rows, width), blocks[0].dtype)] * 3,
        in_specs=in_vmem(chips),
        out_specs=in_vmem(3),
        name="join",
    )(*[resident(b) for b in blocks])


def scores_of(q, k_ref, columns):
    return lax.dot_general(
        q, k_ref[:, columns], (((1,), (1,)), ((), ())), preferred_element_type=jnp.float32
    )


def near(q_rows, k_own, v_own, k_other, v_other, places):
    length, width = q_rows.shape
    heads = width // HD
    step = min(256, length)
    scale = 1.0 / (math.sqrt(HD) * math.log(2.0))

    def body(q_all, ko, vo, kt, vt, at, top_ref, sum_ref, acc_ref):
        core = lax.axis_index("sp") % CORES
        own = at[pl.ds(core, 1), :]
        other = at[pl.ds(1 - core, 1), :]

        def chunk(index):
            start = pl.multiple_of(index * step, step)
            here = pl.ds(start, step)
            row = own if step == length else at[pl.ds(core, 1), here]
            order = jnp.transpose(jnp.broadcast_to(row, (HD, step)))[:, :1]
            for head in range(heads):
                columns = slice(head * HD, (head + 1) * HD)
                q = q_all[here, columns]
                first = jnp.where(own <= order, scores_of(q, ko, columns), NEG)
                second = jnp.where(other <= order, scores_of(q, kt, columns), NEG)
                top = jnp.maximum(
                    jnp.max(first, axis=1, keepdims=True), jnp.max(second, axis=1, keepdims=True)
                )
                first = jnp.exp2((first - top) * scale)
                second = jnp.exp2((second - top) * scale)
                total = jnp.sum(first, axis=1, keepdims=True) + jnp.sum(second, axis=1, keepdims=True)
                acc = jnp.dot(
                    first.astype(jnp.bfloat16), vo[:, columns], preferred_element_type=jnp.float32
                ) + jnp.dot(
                    second.astype(jnp.bfloat16), vt[:, columns], preferred_element_type=jnp.float32
                )
                top_ref[head, here, :] = jnp.broadcast_to(top, (step, HD))
                sum_ref[head, here, :] = jnp.broadcast_to(total, (step, HD))
                acc_ref[here, columns] = acc

        if length == step:
            chunk(0)
        else:
            pl.loop(0, length // step)(chunk)

    state = pltpu.VMEM((heads, length, HD), jnp.float32)
    return pl.pallas_call(
        body,
        out_shape=[state, state, pltpu.VMEM((length, width), jnp.float32)],
        in_specs=in_vmem(6),
        out_specs=in_vmem(3),
        compiler_params=pltpu.CompilerParams(vmem_limit_bytes=VMEM_LIMIT),
        cost_estimate=pl.CostEstimate(
            flops=8 * length * length * width, bytes_accessed=0, transcendentals=2 * length * length * heads
        ),
        name="near",
    )(*[resident(x) for x in (q_rows, k_own, v_own, k_other, v_other)], places)


def far(q_all, top_in, sum_in, acc_in, k_own, v_own, k_other, v_other, skip, chips):
    length, width = q_all.shape
    rows, heads = length // chips, width // HD
    step = min(256, length)
    scale = 1.0 / (math.sqrt(HD) * math.log(2.0))

    def body(skip_ref, q_ref, top_ref, sum_ref, acc_ref, ko, vo, kt, vt, *rest):
        out_refs, done = rest[:chips], rest[chips]
        chip = lax.axis_index("sp") // CORES
        hidden = skip_ref[0] != 0

        def chunk(index):
            here = pl.ds(pl.multiple_of(index * step, step), step)
            for head in range(heads):
                columns = slice(head * HD, (head + 1) * HD)
                q = q_ref[here, columns]
                first = jnp.where(hidden, NEG, scores_of(q, ko, columns))
                second = jnp.where(hidden, NEG, scores_of(q, kt, columns))
                old = top_ref[head, here, :][:, :1]
                top = jnp.maximum(
                    old,
                    jnp.maximum(
                        jnp.max(first, axis=1, keepdims=True), jnp.max(second, axis=1, keepdims=True)
                    ),
                )
                keep = jnp.exp2((old - top) * scale)
                first = jnp.exp2((first - top) * scale)
                second = jnp.exp2((second - top) * scale)
                total = (
                    keep * sum_ref[head, here, :][:, :1]
                    + jnp.sum(first, axis=1, keepdims=True)
                    + jnp.sum(second, axis=1, keepdims=True)
                )
                acc = (
                    keep * acc_ref[here, columns]
                    + jnp.dot(first.astype(jnp.bfloat16), vo[:, columns], preferred_element_type=jnp.float32)
                    + jnp.dot(second.astype(jnp.bfloat16), vt[:, columns], preferred_element_type=jnp.float32)
                )
                done[here, columns] = (acc / total).astype(jnp.bfloat16)

        if length == step:
            chunk(0)
        else:
            pl.loop(0, length // step)(chunk)
        for flip, out in enumerate(out_refs):
            out[...] = done[pl.ds(pl.multiple_of((chip ^ flip) * rows, rows), rows), :]

    return pl.pallas_call(
        body,
        out_shape=[pltpu.VMEM((rows, width), jnp.bfloat16)] * chips,
        in_specs=[pl.BlockSpec(memory_space=pltpu.SMEM)] + in_vmem(8),
        out_specs=in_vmem(chips),
        scratch_shapes=[pltpu.VMEM((length, width), jnp.bfloat16)],
        compiler_params=pltpu.CompilerParams(vmem_limit_bytes=VMEM_LIMIT),
        cost_estimate=pl.CostEstimate(
            flops=8 * length * length * width, bytes_accessed=0, transcendentals=2 * length * length * heads
        ),
        name="far",
    )(skip, *[resident(x) for x in (q_all, top_in, sum_in, acc_in, k_own, v_own, k_other, v_other)])


def unpack(blocks):
    chips = len(blocks)
    rows, width = blocks[0].shape

    def body(*refs):
        block_refs, out_ref, sems = refs[:chips], refs[chips], refs[-1]
        chip = lax.axis_index("sp") // CORES
        copies = []
        for flip, block in enumerate(block_refs):
            columns = pl.ds(pl.multiple_of((chip ^ flip) * width, HD), width)
            copies.append(pltpu.make_async_copy(block, out_ref.at[0, :, columns], sems.at[flip]))
        for copy in copies:
            copy.start()
        for copy in copies:
            copy.wait()

    return pl.pallas_call(
        body,
        out_shape=jax.ShapeDtypeStruct((1, rows, chips * width), blocks[0].dtype),
        in_specs=in_vmem(chips),
        out_specs=pl.BlockSpec(memory_space=pl.ANY),
        scratch_shapes=[pltpu.SemaphoreType.DMA((chips,))],
        name="unpack",
    )(*[resident(b) for b in blocks])


def on_device(queries, keys, values, positions, anchor):
    groups, chips = lax.axis_size("grp"), lax.axis_size("sp") // CORES
    bits = groups.bit_length() - 1
    root, group = anchor[0] % groups, lax.axis_index("grp")
    rows = queries.shape[1]

    blocks = pack(queries, keys, values, chips)
    blocks = [blocks[0]] + [swap(blocks[f], "sp", CORES * f) for f in range(1, chips)]
    q_rows, k_own, v_own = join(blocks)

    k_far, v_far = k_own, v_own
    for stage in range(bits):
        for which in range(2):
            bit = stage if which == 0 else bits - 1 - stage
            mine = ((root >> bit) & 1) == ((group >> bit) & 1)
            if which == 0:
                k_far = jnp.where(mine, k_far, swap(k_far, "grp", 1 << bit))
            else:
                v_far = jnp.where(mine, v_far, swap(v_far, "grp", 1 << bit))
    k_other, v_other = swap(k_own, "sp", 1), swap(v_own, "sp", 1)
    k_far_other, v_far_other = swap(k_far, "sp", 1), swap(v_far, "sp", 1)

    places = jnp.swapaxes(positions.reshape(chips, CORES, rows), 0, 1).reshape(CORES, chips * rows)
    top, total, acc = near(q_rows, k_own, v_own, k_other, v_other, places)
    skip = (group == root).astype(jnp.int32).reshape(1)
    done = far(q_rows, top, total, acc, k_far, v_far, k_far_other, v_far_other, skip, chips)
    back = [done[0]] + [swap(done[f], "sp", CORES * f) for f in range(1, chips)]
    return unpack(back)


def solution(mesh):
    return jax.shard_map(
        on_device,
        mesh=mesh,
        in_specs=(
            P("grp", "sp", None),
            P("grp", "sp", None),
            P("grp", "sp", None),
            P("grp", None),
            P(),
        ),
        out_specs=P("grp", "sp", None),
        check_vma=False,
    )
```

```python
import math

import jax
import jax.numpy as jnp
from jax import lax
from jax.experimental import pallas as pl
from jax.experimental.pallas import tpu as pltpu
from jax.sharding import PartitionSpec as P

HD = 128
CORES = 2
NEG = -1e30
EXP_SCALE = 1.0 / (math.sqrt(HD) * math.log(2.0))
VMEM_LIMIT = 48 * 2**20
ANY = pl.BlockSpec(memory_space=pl.ANY)
SMEM = pl.BlockSpec(memory_space=pltpu.SMEM)


def in_vmem(count):
    return [pl.BlockSpec(memory_space=pltpu.VMEM)] * count


def resident(*arrays):
    return [pltpu.with_memory_space_constraint(x, pltpu.VMEM) for x in arrays]


def swap(x, flip):
    return lax.ppermute(x, "sp", [(i, i ^ flip) for i in range(lax.axis_size("sp"))])


def pack(queries, keys, values):
    chips = lax.axis_size("sp") // CORES
    rows, width = queries.shape[1], queries.shape[2] // chips

    def body(q_ref, k_ref, v_ref, *rest):
        qk_refs, v_refs, sems = rest[:chips], rest[chips : 2 * chips], rest[-1]
        chip = lax.axis_index("sp") // CORES
        copies = []
        for flip in reversed(range(chips)):
            columns = pl.ds(pl.multiple_of((chip ^ flip) * width, HD), width)
            targets = (qk_refs[flip].at[0], qk_refs[flip].at[1], v_refs[flip])
            for part, source in enumerate((q_ref, k_ref, v_ref)):
                copies.append(
                    pltpu.make_async_copy(
                        source.at[0, :, columns], targets[part], sems.at[3 * flip + part]
                    )
                )
        for copy in copies:
            copy.start()
        for copy in copies:
            copy.wait()

    outs = pl.pallas_call(
        body,
        out_shape=[pltpu.VMEM((2, rows, width), keys.dtype)] * chips
        + [pltpu.VMEM((rows, width), values.dtype)] * chips,
        in_specs=[ANY] * 3,
        out_specs=in_vmem(2 * chips),
        scratch_shapes=[pltpu.SemaphoreType.DMA((3 * chips,))],
        name="pack",
    )(queries, keys, values)
    return outs[:chips], outs[chips:]


def join(blocks, after=()):
    chips, parts = len(blocks), blocks[0].shape[:-2]
    rows, width = blocks[0].shape[-2:]
    count = parts[0] if parts else 1

    def body(*refs):
        for flip, block in zip(reversed(range(chips)), refs[:chips]):
            for part, out in enumerate(refs[chips + len(after) :]):
                out[chip_rows(flip, rows), :] = block[part] if parts else block[...]

    return pl.pallas_call(
        body,
        out_shape=[pltpu.VMEM((chips * rows, width), blocks[0].dtype)] * count,
        in_specs=in_vmem(chips + len(after)),
        out_specs=in_vmem(count),
        name="join",
    )(*resident(*reversed(blocks), *after))


def chip_rows(flip, rows):
    chip = lax.axis_index("sp") // CORES
    return pl.ds(pl.multiple_of((chip ^ flip) * rows, rows), rows)


def turn(x, bit):
    return lax.ppermute(x, "grp", [(i, i ^ (1 << bit)) for i in range(lax.axis_size("grp"))])


def choose(mine, theirs, anchor, bit, after=()):
    def body(anchor_ref, mine_ref, theirs_ref, *rest):
        out_ref = rest[-1]
        same = ((anchor_ref[0] % lax.axis_size("grp") ^ lax.axis_index("grp")) >> bit) & 1

        @pl.when(same == 0)
        def _():
            out_ref[...] = mine_ref[...]

        @pl.when(same != 0)
        def _():
            out_ref[...] = theirs_ref[...]

    return pl.pallas_call(
        body,
        out_shape=pltpu.VMEM(mine.shape, mine.dtype),
        in_specs=[SMEM] + in_vmem(2 + len(after)),
        out_specs=in_vmem(1)[0],
        name="choose",
    )(anchor, *resident(mine, theirs, *after))


def scores_of(q, k_ref, columns):
    return lax.dot_general(
        q, k_ref[:, columns], (((1,), (1,)), ((), ())), preferred_element_type=jnp.float32
    )


def mix(weights, v_ref, columns):
    return jnp.dot(
        weights.astype(jnp.bfloat16), v_ref[:, columns], preferred_element_type=jnp.float32
    )


def each_chunk(length, chunk):
    step = min(256, length)
    if length == step:
        chunk(0, step)
    else:
        pl.loop(0, length // step)(lambda index: chunk(pl.multiple_of(index * step, step), step))


def cost(length, width):
    return pl.CostEstimate(
        flops=8 * length * length * width,
        bytes_accessed=0,
        transcendentals=2 * length * length * (width // HD),
    )


def attend(q, own_k, own_v, other_k, other_v, columns, own_mask, other_mask, before):
    first = own_mask(scores_of(q, own_k, columns))
    second = other_mask(scores_of(q, other_k, columns))
    top = jnp.maximum(jnp.max(first, axis=1, keepdims=True), jnp.max(second, axis=1, keepdims=True))
    if before is not None:
        top = jnp.maximum(top, before[0])
    first = jnp.exp2((first - top) * EXP_SCALE)
    second = jnp.exp2((second - top) * EXP_SCALE)
    total = jnp.sum(first, axis=1, keepdims=True) + jnp.sum(second, axis=1, keepdims=True)
    acc = mix(first, own_v, columns) + mix(second, other_v, columns)
    if before is not None:
        keep = jnp.exp2((before[0] - top) * EXP_SCALE)
        total, acc = keep * before[1] + total, keep * before[2] + acc
    return top, total, acc


def near(q_rows, own, other, positions):
    length, width = q_rows.shape
    chips = lax.axis_size("sp") // CORES
    rows = length // chips
    paired = CORES * rows == HD and chips % 2 == 0
    if not paired:
        positions = jnp.swapaxes(positions.reshape(chips, CORES, rows), 0, 1).reshape(CORES, length)

    def split(at):
        if not paired:
            return [jnp.broadcast_to(at[c : c + 1, :], (8, length)) for c in range(CORES)]
        low = lax.broadcasted_iota(jnp.int32, (8, HD), 1) < rows
        tokens = [jnp.broadcast_to(at[:, c * HD : (c + 1) * HD], (8, HD)) for c in range(chips)]
        turned = [pltpu.roll(row, rows, 1) for row in tokens]
        pairs = range(0, chips, 2)
        return [
            jnp.concatenate([jnp.where(low, tokens[c], turned[c + 1]) for c in pairs], 1),
            jnp.concatenate([jnp.where(low, turned[c], tokens[c + 1]) for c in pairs], 1),
        ]

    def body(q_ref, own_k, own_v, other_k, other_v, at, top_ref, sum_ref, acc_ref, end_ref, own_at):
        end_ref[...] = jnp.zeros_like(end_ref)
        core = lax.axis_index("sp") % CORES
        first_at, second_at = split(at)
        own_at[...] = jnp.where(core == 0, first_at, second_at)
        other_at = jnp.where(core == 0, second_at, first_at)[:1, :]

        def chunk(start, step):
            here = pl.ds(start, step)
            order = jnp.transpose(jnp.broadcast_to(own_at[:1, here], (HD, step)))[:, :1]
            for head in range(width // HD):
                columns = slice(head * HD, (head + 1) * HD)
                top, total, acc = attend(
                    q_ref[here, columns],
                    own_k,
                    own_v,
                    other_k,
                    other_v,
                    columns,
                    lambda scores: jnp.where(own_at[:1, :] <= order, scores, NEG),
                    lambda scores: jnp.where(other_at <= order, scores, NEG),
                    None,
                )
                top_ref[head, here, :] = jnp.broadcast_to(top, (step, HD))
                sum_ref[head, here, :] = jnp.broadcast_to(total, (step, HD))
                acc_ref[here, columns] = acc

        each_chunk(length, chunk)

    state = pltpu.VMEM((width // HD, length, HD), jnp.float32)
    return pl.pallas_call(
        body,
        out_shape=[
            state,
            state,
            pltpu.VMEM((length, width), jnp.float32),
            pltpu.VMEM((8, HD), jnp.float32),
        ],
        in_specs=in_vmem(6),
        out_specs=in_vmem(4),
        scratch_shapes=[pltpu.VMEM((8, length), jnp.int32)],
        compiler_params=pltpu.CompilerParams(vmem_limit_bytes=VMEM_LIMIT),
        cost_estimate=cost(length, width),
        name="near",
    )(*resident(q_rows, *own, *other), positions)


def far(q_rows, state, own, other, anchor):
    length, width = q_rows.shape
    chips = lax.axis_size("sp") // CORES
    rows = length // chips

    def body(anchor_ref, q_ref, top_ref, sum_ref, acc_ref, own_k, own_v, other_k, other_v, *rest):
        out_refs, done = rest[:chips], rest[chips]
        hidden = lax.axis_index("grp") == anchor_ref[0] % lax.axis_size("grp")

        def mask(scores):
            return jnp.where(hidden, NEG, scores)

        def chunk(start, step):
            here = pl.ds(start, step)
            for head in range(width // HD):
                columns = slice(head * HD, (head + 1) * HD)
                before = (
                    top_ref[head, here, :][:, :1],
                    sum_ref[head, here, :][:, :1],
                    acc_ref[here, columns],
                )
                _, total, acc = attend(
                    q_ref[here, columns], own_k, own_v, other_k, other_v, columns, mask, mask, before
                )
                done[here, columns] = (acc / total).astype(jnp.bfloat16)

        each_chunk(length, chunk)
        for flip, out in zip(reversed(range(chips)), out_refs):
            out[...] = done[chip_rows(flip, rows), :]

    outs = pl.pallas_call(
        body,
        out_shape=[pltpu.VMEM((rows, width), jnp.bfloat16)] * chips,
        in_specs=[SMEM] + in_vmem(8),
        out_specs=in_vmem(chips),
        scratch_shapes=[pltpu.VMEM((length, width), jnp.bfloat16)],
        compiler_params=pltpu.CompilerParams(vmem_limit_bytes=VMEM_LIMIT),
        cost_estimate=cost(length, width),
        name="far",
    )(anchor, *resident(q_rows, *state, *own, *other))
    return outs[::-1]


def unpack(blocks):
    chips = len(blocks)
    rows, width = blocks[0].shape

    def body(*refs):
        block_refs, out_ref, sems = refs[:chips], refs[chips], refs[-1]
        chip = lax.axis_index("sp") // CORES
        copies = []
        for flip, block in zip(reversed(range(chips)), block_refs):
            columns = pl.ds(pl.multiple_of((chip ^ flip) * width, HD), width)
            copies.append(pltpu.make_async_copy(block, out_ref.at[0, :, columns], sems.at[flip]))
        for copy in copies:
            copy.start()
        for copy in copies:
            copy.wait()

    return pl.pallas_call(
        body,
        out_shape=jax.ShapeDtypeStruct((1, rows, chips * width), blocks[0].dtype),
        in_specs=in_vmem(chips),
        out_specs=ANY,
        scratch_shapes=[pltpu.SemaphoreType.DMA((chips,))],
        name="unpack",
    )(*resident(*reversed(blocks)))


def trade(blocks):
    moved = {flip: swap(blocks[flip], CORES * flip) for flip in reversed(range(1, len(blocks)))}
    return [blocks[0]] + [moved[flip] for flip in range(1, len(blocks))]


def on_device(queries, keys, values, positions, anchor):
    qk_blocks, v_blocks = pack(queries, keys, values)
    q_rows, k_own = join(trade(qk_blocks))
    (v_own,) = join(trade(v_blocks), [q_rows])
    own = k_own, v_own
    other = [swap(x, 1) for x in own]
    *state, end = near(q_rows, own, other, positions)

    bits = lax.axis_size("grp").bit_length() - 1
    k_far, v_far = own
    for stage in range(bits):
        after = [end] if stage == 1 else ()
        k_far = choose(k_far, turn(k_far, stage), anchor, stage, after)
        back = bits - 1 - stage
        v_far = choose(v_far, turn(v_far, back), anchor, back)
    other = [swap(x, 1) for x in (k_far, v_far)]
    return unpack(trade(far(q_rows, state, (k_far, v_far), other, anchor)))


def solution(mesh):
    return jax.shard_map(
        on_device,
        mesh=mesh,
        in_specs=(
            P("grp", "sp", None),
            P("grp", "sp", None),
            P("grp", "sp", None),
            P("grp", None),
            P(),
        ),
        out_specs=P("grp", "sp", None),
        check_vma=False,
    )
```

```python
import math

import jax
import jax.numpy as jnp
from jax import lax
from jax.experimental import pallas as pl
from jax.experimental.pallas import tpu as pltpu
from jax.sharding import PartitionSpec as P

HD = 128
CORES = 2
NEG = -1e30
EXP_SCALE = 1.0 / (math.sqrt(HD) * math.log(2.0))
VMEM_LIMIT = 48 * 2**20
ANY = pl.BlockSpec(memory_space=pl.ANY)
SMEM = pl.BlockSpec(memory_space=pltpu.SMEM)


def in_vmem(count):
    return [pl.BlockSpec(memory_space=pltpu.VMEM)] * count


def resident(*arrays):
    return [pltpu.with_memory_space_constraint(x, pltpu.VMEM) for x in arrays]


def swap(x, flip):
    return lax.ppermute(x, "sp", [(i, i ^ flip) for i in range(lax.axis_size("sp"))])


def pack(queries, keys, values):
    chips = lax.axis_size("sp") // CORES
    rows, width = queries.shape[1], queries.shape[2] // chips

    def body(q_ref, k_ref, v_ref, *rest):
        qk_refs, v_refs, sems = rest[:chips], rest[chips : 2 * chips], rest[-1]
        chip = lax.axis_index("sp") // CORES
        copies = []
        for flip in reversed(range(chips)):
            columns = pl.ds(pl.multiple_of((chip ^ flip) * width, HD), width)
            targets = (qk_refs[flip].at[0], qk_refs[flip].at[1], v_refs[flip])
            for part, source in enumerate((q_ref, k_ref, v_ref)):
                copies.append(
                    pltpu.make_async_copy(
                        source.at[0, :, columns], targets[part], sems.at[3 * flip + part]
                    )
                )
        for copy in copies:
            copy.start()
        for copy in copies:
            copy.wait()

    outs = pl.pallas_call(
        body,
        out_shape=[pltpu.VMEM((2, rows, width), keys.dtype)] * chips
        + [pltpu.VMEM((rows, width), values.dtype)] * chips,
        in_specs=[ANY] * 3,
        out_specs=in_vmem(2 * chips),
        scratch_shapes=[pltpu.SemaphoreType.DMA((3 * chips,))],
        name="pack",
    )(queries, keys, values)
    return outs[:chips], outs[chips:]


def join(blocks, order, after=()):
    chips, parts = len(blocks), blocks[0].shape[:-2]
    rows, width = blocks[0].shape[-2:]
    count = parts[0] if parts else 1

    def body(*refs):
        for flip, block in zip((*order, 0), refs[:chips]):
            for part, out in enumerate(refs[chips + len(after) :]):
                out[chip_rows(flip, rows), :] = block[part] if parts else block[...]

    return pl.pallas_call(
        body,
        out_shape=[pltpu.VMEM((chips * rows, width), blocks[0].dtype)] * count,
        in_specs=in_vmem(chips + len(after)),
        out_specs=in_vmem(count),
        name="join",
    )(*resident(*[blocks[flip] for flip in (*order, 0)], *after))


def chip_rows(flip, rows):
    chip = lax.axis_index("sp") // CORES
    return pl.ds(pl.multiple_of((chip ^ flip) * rows, rows), rows)


def turn(x, bit):
    return lax.ppermute(x, "grp", [(i, i ^ (1 << bit)) for i in range(lax.axis_size("grp"))])


def choose(mine, theirs, anchor, bit, after=()):
    def body(anchor_ref, mine_ref, theirs_ref, *rest):
        out_ref = rest[-1]
        same = ((anchor_ref[0] % lax.axis_size("grp") ^ lax.axis_index("grp")) >> bit) & 1

        @pl.when(same == 0)
        def _():
            out_ref[...] = mine_ref[...]

        @pl.when(same != 0)
        def _():
            out_ref[...] = theirs_ref[...]

    return pl.pallas_call(
        body,
        out_shape=pltpu.VMEM(mine.shape, mine.dtype),
        in_specs=[SMEM] + in_vmem(2 + len(after)),
        out_specs=in_vmem(1)[0],
        name="choose",
    )(anchor, *resident(mine, theirs, *after))


def scores_of(q, k_ref, columns):
    return lax.dot_general(
        q, k_ref[:, columns], (((1,), (1,)), ((), ())), preferred_element_type=jnp.float32
    )


def mix(weights, v_ref, columns):
    return jnp.dot(weights, v_ref[:, columns], preferred_element_type=jnp.float32)


def each_chunk(length, chunk):
    step = min(256, length)
    if length == step:
        chunk(0, step)
    else:
        pl.loop(0, length // step)(lambda index: chunk(pl.multiple_of(index * step, step), step))


def cost(length, width):
    return pl.CostEstimate(
        flops=8 * length * length * width,
        bytes_accessed=0,
        transcendentals=2 * length * length * (width // HD),
    )


def weigh(q, own_k, other_k, columns, own_mask, other_mask, before=None):
    first = own_mask(scores_of(q, own_k, columns))
    second = other_mask(scores_of(q, other_k, columns))
    top = jnp.maximum(jnp.max(first, axis=1, keepdims=True), jnp.max(second, axis=1, keepdims=True))
    if before is not None:
        top = jnp.maximum(top, before)
    first = jnp.exp2((first - top) * EXP_SCALE)
    second = jnp.exp2((second - top) * EXP_SCALE)
    total = jnp.sum(first, axis=1, keepdims=True) + jnp.sum(second, axis=1, keepdims=True)
    return first.astype(jnp.bfloat16), second.astype(jnp.bfloat16), top, total


def near(q_rows, own, other, positions):
    length, width = q_rows.shape
    chips = lax.axis_size("sp") // CORES
    rows = length // chips
    paired = CORES * rows == HD and chips % 2 == 0
    if not paired:
        positions = jnp.swapaxes(positions.reshape(chips, CORES, rows), 0, 1).reshape(CORES, length)

    def split(at):
        if not paired:
            return [jnp.broadcast_to(at[c : c + 1, :], (8, length)) for c in range(CORES)]
        low = lax.broadcasted_iota(jnp.int32, (8, HD), 1) < rows
        tokens = [jnp.broadcast_to(at[:, c * HD : (c + 1) * HD], (8, HD)) for c in range(chips)]
        turned = [pltpu.roll(row, rows, 1) for row in tokens]
        pairs = range(0, chips, 2)
        return [
            jnp.concatenate([jnp.where(low, tokens[c], turned[c + 1]) for c in pairs], 1),
            jnp.concatenate([jnp.where(low, turned[c], tokens[c + 1]) for c in pairs], 1),
        ]

    def body(q_ref, own_k, own_v, other_k, other_v, at, top_ref, sum_ref, acc_ref, end_ref, own_at):
        end_ref[...] = jnp.zeros_like(end_ref)
        core = lax.axis_index("sp") % CORES
        first_at, second_at = split(at)
        own_at[...] = jnp.where(core == 0, first_at, second_at)
        other_at = jnp.where(core == 0, second_at, first_at)[:1, :]

        def chunk(start, step):
            here = pl.ds(start, step)
            order = jnp.transpose(jnp.broadcast_to(own_at[:1, here], (HD, step)))[:, :1]
            for head in range(width // HD):
                columns = slice(head * HD, (head + 1) * HD)
                first, second, top, total = weigh(
                    q_ref[here, columns],
                    own_k,
                    other_k,
                    columns,
                    lambda scores: jnp.where(own_at[:1, :] <= order, scores, NEG),
                    lambda scores: jnp.where(other_at <= order, scores, NEG),
                )
                top_ref[head, here, :] = jnp.broadcast_to(top, (step, HD))
                sum_ref[head, here, :] = jnp.broadcast_to(total, (step, HD))
                acc_ref[here, columns] = mix(first, own_v, columns) + mix(second, other_v, columns)

        each_chunk(length, chunk)

    state = pltpu.VMEM((width // HD, length, HD), jnp.float32)
    return pl.pallas_call(
        body,
        out_shape=[
            state,
            state,
            pltpu.VMEM((length, width), jnp.float32),
            pltpu.VMEM((8, HD), jnp.float32),
        ],
        in_specs=in_vmem(6),
        out_specs=in_vmem(4),
        scratch_shapes=[pltpu.VMEM((8, length), jnp.int32)],
        compiler_params=pltpu.CompilerParams(vmem_limit_bytes=VMEM_LIMIT),
        cost_estimate=cost(length, width),
        name="near",
    )(*resident(q_rows, *own, *other), positions)


def far_weights(q_rows, top, own_k, other_k, anchor):
    length, width = q_rows.shape
    heads = width // HD

    def body(anchor_ref, q_ref, old_ref, own_k, other_k, first_ref, second_ref, top_ref, sum_ref):
        hidden = lax.axis_index("grp") == anchor_ref[0] % lax.axis_size("grp")

        def mask(scores):
            return jnp.where(hidden, NEG, scores)

        def chunk(start, step):
            here = pl.ds(start, step)
            for head in range(heads):
                columns = slice(head * HD, (head + 1) * HD)
                old = old_ref[head, here, :][:, :1]
                first, second, top, total = weigh(
                    q_ref[here, columns], own_k, other_k, columns, mask, mask, old
                )
                first_ref[head, here, :] = first
                second_ref[head, here, :] = second
                top_ref[head, here, :] = jnp.broadcast_to(top, (step, HD))
                sum_ref[head, here, :] = jnp.broadcast_to(total, (step, HD))

        each_chunk(length, chunk)

    weights = pltpu.VMEM((heads, length, length), jnp.bfloat16)
    state = pltpu.VMEM((heads, length, HD), jnp.float32)
    return pl.pallas_call(
        body,
        out_shape=[weights, weights, state, state],
        in_specs=[SMEM] + in_vmem(4),
        out_specs=in_vmem(4),
        compiler_params=pltpu.CompilerParams(vmem_limit_bytes=VMEM_LIMIT),
        cost_estimate=cost(length, width),
        name="far_weights",
    )(anchor, *resident(q_rows, top, own_k, other_k))


def far_values(near_state, far_state, own_v, other_v):
    length, width = near_state[-1].shape
    chips = lax.axis_size("sp") // CORES
    rows = length // chips

    def body(*refs):
        old_top, old_sum, old_acc, first_ref, second_ref, top_ref, sum_ref, own_v, other_v = refs[:9]
        out_refs, done = refs[9:-1], refs[-1]

        def chunk(start, step):
            here = pl.ds(start, step)
            for head in range(width // HD):
                columns = slice(head * HD, (head + 1) * HD)
                keep = jnp.exp2((old_top[head, here, :] - top_ref[head, here, :]) * EXP_SCALE)
                total = keep * old_sum[head, here, :] + sum_ref[head, here, :]
                acc = (
                    keep * old_acc[here, columns]
                    + mix(first_ref[head, here, :], own_v, columns)
                    + mix(second_ref[head, here, :], other_v, columns)
                )
                done[here, columns] = (acc / total).astype(jnp.bfloat16)

        each_chunk(length, chunk)
        for flip, out in enumerate(out_refs):
            out[...] = done[chip_rows(flip, rows), :]

    return pl.pallas_call(
        body,
        out_shape=[pltpu.VMEM((rows, width), jnp.bfloat16)] * chips,
        in_specs=in_vmem(9),
        out_specs=in_vmem(chips),
        scratch_shapes=[pltpu.VMEM((length, width), jnp.bfloat16)],
        compiler_params=pltpu.CompilerParams(vmem_limit_bytes=VMEM_LIMIT),
        cost_estimate=cost(length, width),
        name="far_values",
    )(*resident(*near_state, *far_state, own_v, other_v))


def unpack(blocks, order):
    chips = len(blocks)
    rows, width = blocks[0].shape

    def body(*refs):
        block_refs, out_ref, sems = refs[:chips], refs[chips], refs[-1]
        chip = lax.axis_index("sp") // CORES
        copies = []
        for flip, block in zip((*order, 0), block_refs):
            columns = pl.ds(pl.multiple_of((chip ^ flip) * width, HD), width)
            copies.append(pltpu.make_async_copy(block, out_ref.at[0, :, columns], sems.at[flip]))
        for copy in copies:
            copy.start()
        for copy in copies:
            copy.wait()

    return pl.pallas_call(
        body,
        out_shape=jax.ShapeDtypeStruct((1, rows, chips * width), blocks[0].dtype),
        in_specs=in_vmem(chips),
        out_specs=ANY,
        scratch_shapes=[pltpu.SemaphoreType.DMA((chips,))],
        name="unpack",
    )(*resident(*[blocks[flip] for flip in (*order, 0)]))


def trade(blocks, order):
    moved = {flip: swap(blocks[flip], CORES * flip) for flip in order}
    return [blocks[0]] + [moved[flip] for flip in range(1, len(blocks))]


def on_device(queries, keys, values, positions, anchor):
    order = tuple(reversed(range(1, lax.axis_size("sp") // CORES)))
    qk_blocks, v_blocks = pack(queries, keys, values)
    q_rows, k_own = join(trade(qk_blocks, order), order)
    (v_own,) = join(trade(v_blocks, order), order, [q_rows])
    own = k_own, v_own
    other = [swap(x, 1) for x in own]
    *state, end = near(q_rows, own, other, positions)

    bits = lax.axis_size("grp").bit_length() - 1
    k_far, v_far = own
    for stage in range(bits):
        after = [end] if stage == 1 else ()
        k_far = choose(k_far, turn(k_far, stage), anchor, stage, after)
        back = bits - 1 - stage
        v_far = choose(v_far, turn(v_far, back), anchor, back)
    far_state = far_weights(q_rows, state[0], k_far, swap(k_far, 1), anchor)
    done = far_values(state, far_state, v_far, swap(v_far, 1))
    return unpack(trade(done, order), order)


def solution(mesh):
    return jax.shard_map(
        on_device,
        mesh=mesh,
        in_specs=(
            P("grp", "sp", None),
            P("grp", "sp", None),
            P("grp", "sp", None),
            P("grp", None),
            P(),
        ),
        out_specs=P("grp", "sp", None),
        check_vma=False,
    )
```

```python
import math

import jax
import jax.numpy as jnp
from jax import lax
from jax.experimental import pallas as pl
from jax.experimental.pallas import tpu as pltpu
from jax.sharding import PartitionSpec as P

HD = 128
CORES = 2
NEG = -1e30
EXP_SCALE = 1.0 / (math.sqrt(HD) * math.log(2.0))
VMEM_LIMIT = 48 * 2**20
QUERY_FLOPS = 10**10
ANY = pl.BlockSpec(memory_space=pl.ANY)
SMEM = pl.BlockSpec(memory_space=pltpu.SMEM)


def in_vmem(count):
    return [pl.BlockSpec(memory_space=pltpu.VMEM)] * count


def resident(*arrays):
    return [pltpu.with_memory_space_constraint(x, pltpu.VMEM) for x in arrays]


def swap(x, flip):
    return lax.ppermute(x, "sp", [(i, i ^ flip) for i in range(lax.axis_size("sp"))])


def pack(queries, keys, values):
    chips = lax.axis_size("sp") // CORES
    rows, width = queries.shape[1], queries.shape[2] // chips

    def body(q_ref, k_ref, v_ref, *rest):
        kv_refs, q_refs, sems = rest[:chips], rest[chips : 2 * chips], rest[-1]
        chip = lax.axis_index("sp") // CORES
        copies = []
        for flip in reversed(range(chips)):
            columns = pl.ds(pl.multiple_of((chip ^ flip) * width, HD), width)
            targets = (kv_refs[flip].at[0], kv_refs[flip].at[1], q_refs[flip])
            for part, source in enumerate((k_ref, v_ref, q_ref)):
                copies.append(
                    pltpu.make_async_copy(
                        source.at[0, :, columns], targets[part], sems.at[3 * flip + part]
                    )
                )
        for copy in copies:
            copy.start()
        for copy in copies:
            copy.wait()

    outs = pl.pallas_call(
        body,
        out_shape=[pltpu.VMEM((2, rows, width), keys.dtype)] * chips
        + [pltpu.VMEM((rows, width), values.dtype)] * chips,
        in_specs=[ANY] * 3,
        out_specs=in_vmem(2 * chips),
        scratch_shapes=[pltpu.SemaphoreType.DMA((3 * chips,))],
        name="pack",
    )(queries, keys, values)
    return outs[:chips], outs[chips:]


def join(blocks, order, flops=0):
    chips, parts = len(blocks), blocks[0].shape[:-2]
    rows, width = blocks[0].shape[-2:]
    count = parts[0] if parts else 1

    def body(*refs):
        for flip, block in zip((*order, 0), refs[:chips]):
            for part, out in enumerate(refs[chips:]):
                out[chip_rows(flip, rows), :] = block[part] if parts else block[...]

    return pl.pallas_call(
        body,
        out_shape=[pltpu.VMEM((chips * rows, width), blocks[0].dtype)] * count,
        in_specs=in_vmem(chips),
        out_specs=in_vmem(count),
        cost_estimate=pl.CostEstimate(flops=flops, bytes_accessed=0, transcendentals=0),
        name="join",
    )(*resident(*[blocks[flip] for flip in (*order, 0)]))


def pair(first, second):
    def body(first_ref, second_ref, out_ref):
        out_ref[0] = first_ref[...]
        out_ref[1] = second_ref[...]

    return pl.pallas_call(
        body,
        out_shape=pltpu.VMEM((2, *first.shape), first.dtype),
        in_specs=in_vmem(2),
        out_specs=in_vmem(1)[0],
        name="pair",
    )(*resident(first, second))


def chip_rows(flip, rows):
    chip = lax.axis_index("sp") // CORES
    return pl.ds(pl.multiple_of((chip ^ flip) * rows, rows), rows)


def turn(x, bit):
    return lax.ppermute(x, "grp", [(i, i ^ (1 << bit)) for i in range(lax.axis_size("grp"))])


def choose(mine, theirs, anchor, bit, after=()):
    def body(anchor_ref, mine_ref, theirs_ref, *rest):
        out_ref = rest[-1]
        same = ((anchor_ref[0] % lax.axis_size("grp") ^ lax.axis_index("grp")) >> bit) & 1

        @pl.when(same == 0)
        def _():
            out_ref[...] = mine_ref[...]

        @pl.when(same != 0)
        def _():
            out_ref[...] = theirs_ref[...]

    return pl.pallas_call(
        body,
        out_shape=pltpu.VMEM(mine.shape, mine.dtype),
        in_specs=[SMEM] + in_vmem(2 + len(after)),
        out_specs=in_vmem(1)[0],
        name="choose",
    )(anchor, *resident(mine, theirs, *after))


def scores_of(q, k_ref, columns):
    return lax.dot_general(
        q, k_ref[:, columns], (((1,), (1,)), ((), ())), preferred_element_type=jnp.float32
    )


def mix(weights, v_ref, columns):
    return jnp.dot(weights, v_ref[:, columns], preferred_element_type=jnp.float32)


def each_chunk(length, chunk):
    step = min(256, length)
    if length == step:
        chunk(0, step)
    else:
        pl.loop(0, length // step)(lambda index: chunk(pl.multiple_of(index * step, step), step))


def cost(length, width):
    return pl.CostEstimate(
        flops=8 * length * length * width,
        bytes_accessed=0,
        transcendentals=2 * length * length * (width // HD),
    )


def weigh(q, own_k, other_k, columns, own_mask, other_mask, before=None):
    first = own_mask(scores_of(q, own_k, columns))
    second = other_mask(scores_of(q, other_k, columns))
    top = jnp.maximum(jnp.max(first, axis=1, keepdims=True), jnp.max(second, axis=1, keepdims=True))
    if before is not None:
        top = jnp.maximum(top, before)
    first = jnp.exp2((first - top) * EXP_SCALE)
    second = jnp.exp2((second - top) * EXP_SCALE)
    total = jnp.sum(first, axis=1, keepdims=True) + jnp.sum(second, axis=1, keepdims=True)
    return first.astype(jnp.bfloat16), second.astype(jnp.bfloat16), top, total


def near(q_rows, own_k, own_v, other, positions):
    length, width = q_rows.shape
    chips = lax.axis_size("sp") // CORES
    rows = length // chips
    paired = CORES * rows == HD and chips % 2 == 0
    if not paired:
        positions = jnp.swapaxes(positions.reshape(chips, CORES, rows), 0, 1).reshape(CORES, length)

    def split(at):
        if not paired:
            return [jnp.broadcast_to(at[c : c + 1, :], (8, length)) for c in range(CORES)]
        low = lax.broadcasted_iota(jnp.int32, (8, HD), 1) < rows
        tokens = [jnp.broadcast_to(at[:, c * HD : (c + 1) * HD], (8, HD)) for c in range(chips)]
        turned = [pltpu.roll(row, rows, 1) for row in tokens]
        pairs = range(0, chips, 2)
        return [
            jnp.concatenate([jnp.where(low, tokens[c], turned[c + 1]) for c in pairs], 1),
            jnp.concatenate([jnp.where(low, turned[c], tokens[c + 1]) for c in pairs], 1),
        ]

    def body(q_ref, own_k, own_v, other_kv, at, top_ref, sum_ref, acc_ref, end_ref, own_at):
        end_ref[...] = jnp.zeros_like(end_ref)
        other_k, other_v = other_kv.at[0], other_kv.at[1]
        core = lax.axis_index("sp") % CORES
        first_at, second_at = split(at)
        own_at[...] = jnp.where(core == 0, first_at, second_at)
        other_at = jnp.where(core == 0, second_at, first_at)[:1, :]

        def chunk(start, step):
            here = pl.ds(start, step)
            order = jnp.transpose(jnp.broadcast_to(own_at[:1, here], (HD, step)))[:, :1]
            for head in range(width // HD):
                columns = slice(head * HD, (head + 1) * HD)
                first, second, top, total = weigh(
                    q_ref[here, columns],
                    own_k,
                    other_k,
                    columns,
                    lambda scores: jnp.where(own_at[:1, :] <= order, scores, NEG),
                    lambda scores: jnp.where(other_at <= order, scores, NEG),
                )
                top_ref[head, here, :] = jnp.broadcast_to(top, (step, HD))
                sum_ref[head, here, :] = jnp.broadcast_to(total, (step, HD))
                acc_ref[here, columns] = mix(first, own_v, columns) + mix(second, other_v, columns)

        each_chunk(length, chunk)

    state = pltpu.VMEM((width // HD, length, HD), jnp.float32)
    return pl.pallas_call(
        body,
        out_shape=[
            state,
            state,
            pltpu.VMEM((length, width), jnp.float32),
            pltpu.VMEM((8, HD), jnp.float32),
        ],
        in_specs=in_vmem(5),
        out_specs=in_vmem(4),
        scratch_shapes=[pltpu.VMEM((8, length), jnp.int32)],
        compiler_params=pltpu.CompilerParams(vmem_limit_bytes=VMEM_LIMIT),
        cost_estimate=cost(length, width),
        name="near",
    )(*resident(q_rows, own_k, own_v, other), positions)


def far_weights(q_rows, top, own_k, other_k, anchor):
    length, width = q_rows.shape
    heads = width // HD

    def body(anchor_ref, q_ref, old_ref, own_k, other_k, first_ref, second_ref, top_ref, sum_ref):
        hidden = lax.axis_index("grp") == anchor_ref[0] % lax.axis_size("grp")

        def mask(scores):
            return jnp.where(hidden, NEG, scores)

        def chunk(start, step):
            here = pl.ds(start, step)
            for head in range(heads):
                columns = slice(head * HD, (head + 1) * HD)
                old = old_ref[head, here, :][:, :1]
                first, second, top, total = weigh(
                    q_ref[here, columns], own_k, other_k, columns, mask, mask, old
                )
                first_ref[head, here, :] = first
                second_ref[head, here, :] = second
                top_ref[head, here, :] = jnp.broadcast_to(top, (step, HD))
                sum_ref[head, here, :] = jnp.broadcast_to(total, (step, HD))

        each_chunk(length, chunk)

    weights = pltpu.VMEM((heads, length, length), jnp.bfloat16)
    state = pltpu.VMEM((heads, length, HD), jnp.float32)
    return pl.pallas_call(
        body,
        out_shape=[weights, weights, state, state],
        in_specs=[SMEM] + in_vmem(4),
        out_specs=in_vmem(4),
        compiler_params=pltpu.CompilerParams(vmem_limit_bytes=VMEM_LIMIT),
        cost_estimate=cost(length, width),
        name="far_weights",
    )(anchor, *resident(q_rows, top, own_k, other_k))


def far_values(near_state, far_state, own_v, other_v):
    length, width = near_state[-1].shape
    chips = lax.axis_size("sp") // CORES
    rows = length // chips

    def body(*refs):
        old_top, old_sum, old_acc, first_ref, second_ref, top_ref, sum_ref, own_v, other_v = refs[:9]
        out_refs, done = refs[9:-1], refs[-1]

        def chunk(start, step):
            here = pl.ds(start, step)
            for head in range(width // HD):
                columns = slice(head * HD, (head + 1) * HD)
                keep = jnp.exp2((old_top[head, here, :] - top_ref[head, here, :]) * EXP_SCALE)
                total = keep * old_sum[head, here, :] + sum_ref[head, here, :]
                acc = (
                    keep * old_acc[here, columns]
                    + mix(first_ref[head, here, :], own_v, columns)
                    + mix(second_ref[head, here, :], other_v, columns)
                )
                done[here, columns] = (acc / total).astype(jnp.bfloat16)

        each_chunk(length, chunk)
        for flip, out in enumerate(out_refs):
            out[...] = done[chip_rows(flip, rows), :]

    return pl.pallas_call(
        body,
        out_shape=[pltpu.VMEM((rows, width), jnp.bfloat16)] * chips,
        in_specs=in_vmem(9),
        out_specs=in_vmem(chips),
        scratch_shapes=[pltpu.VMEM((length, width), jnp.bfloat16)],
        compiler_params=pltpu.CompilerParams(vmem_limit_bytes=VMEM_LIMIT),
        cost_estimate=cost(length, width),
        name="far_values",
    )(*resident(*near_state, *far_state, own_v, other_v))


def unpack(blocks, order):
    chips = len(blocks)
    rows, width = blocks[0].shape

    def body(*refs):
        block_refs, out_ref, sems = refs[:chips], refs[chips], refs[-1]
        chip = lax.axis_index("sp") // CORES
        copies = []
        for flip, block in zip((*order, 0), block_refs):
            columns = pl.ds(pl.multiple_of((chip ^ flip) * width, HD), width)
            copies.append(pltpu.make_async_copy(block, out_ref.at[0, :, columns], sems.at[flip]))
        for copy in copies:
            copy.start()
        for copy in copies:
            copy.wait()

    return pl.pallas_call(
        body,
        out_shape=jax.ShapeDtypeStruct((1, rows, chips * width), blocks[0].dtype),
        in_specs=in_vmem(chips),
        out_specs=ANY,
        scratch_shapes=[pltpu.SemaphoreType.DMA((chips,))],
        name="unpack",
    )(*resident(*[blocks[flip] for flip in (*order, 0)]))


def trade(blocks, order):
    moved = {flip: swap(blocks[flip], CORES * flip) for flip in order}
    return [blocks[0]] + [moved[flip] for flip in range(1, len(blocks))]


def on_device(queries, keys, values, positions, anchor):
    chips = lax.axis_size("sp") // CORES
    distant_first = tuple(reversed(range(1, chips)))
    crossing_first = tuple(sorted(range(1, chips), key=lambda flip: (flip < chips // 2, flip)))

    kv_blocks, q_blocks = pack(queries, keys, values)
    k_own, v_own = join(trade(kv_blocks, crossing_first), crossing_first)
    (q_rows,) = join(trade(q_blocks, distant_first), distant_first, QUERY_FLOPS)
    other = swap(pair(k_own, v_own), 1)

    bits = lax.axis_size("grp").bit_length() - 1
    k_far, v_far, *state, end = k_own, v_own, *near(q_rows, k_own, v_own, other, positions)
    for stage in range(bits):
        after = [[q_rows], [end]][stage] if stage < 2 else ()
        back = bits - 1 - stage
        k_far = choose(k_far, turn(k_far, stage), anchor, stage, after)
        v_far = choose(v_far, turn(v_far, back), anchor, back)
    far_state = far_weights(q_rows, state[0], k_far, swap(k_far, 1), anchor)
    done = far_values(state, far_state, v_far, swap(v_far, 1))
    return unpack(trade(done, distant_first), distant_first)


def solution(mesh):
    return jax.shard_map(
        on_device,
        mesh=mesh,
        in_specs=(
            P("grp", "sp", None),
            P("grp", "sp", None),
            P("grp", "sp", None),
            P("grp", None),
            P(),
        ),
        out_specs=P("grp", "sp", None),
        check_vma=False,
    )
```

```python
import math

import jax
import jax.numpy as jnp
from jax import lax
from jax.experimental import pallas as pl
from jax.experimental.pallas import tpu as pltpu
from jax.sharding import PartitionSpec as P

HD = 128
CORES = 2
NEG = -1e30
EXP_SCALE = 1.0 / (math.sqrt(HD) * math.log(2.0))
VMEM_LIMIT = 48 * 2**20
QUERY_FLOPS = 10**10
ANY = pl.BlockSpec(memory_space=pl.ANY)
SMEM = pl.BlockSpec(memory_space=pltpu.SMEM)


def in_vmem(count):
    return [pl.BlockSpec(memory_space=pltpu.VMEM)] * count


def resident(*arrays):
    return [pltpu.with_memory_space_constraint(x, pltpu.VMEM) for x in arrays]


def swap(x, flip):
    return lax.ppermute(x, "sp", [(i, i ^ flip) for i in range(lax.axis_size("sp"))])


def flip_of(flips):
    return jnp.where(lax.axis_index("sp") % CORES == 0, flips[0], flips[1])


def pack(queries, keys, values, kv_slots, q_slots):
    chips = lax.axis_size("sp") // CORES
    rows, width = queries.shape[1], queries.shape[2] // chips

    def body(q_ref, k_ref, v_ref, *rest):
        kv_refs, q_refs, sems = rest[:chips], rest[chips : 2 * chips], rest[-1]
        chip = lax.axis_index("sp") // CORES
        copies = []
        for slot in reversed(range(chips)):
            targets = (kv_refs[slot].at[0], kv_refs[slot].at[1], q_refs[slot])
            for part, source in enumerate((k_ref, v_ref, q_ref)):
                flip = flip_of((q_slots if part == 2 else kv_slots)[slot])
                columns = pl.ds(pl.multiple_of((chip ^ flip) * width, HD), width)
                copies.append(
                    pltpu.make_async_copy(
                        source.at[0, :, columns], targets[part], sems.at[3 * slot + part]
                    )
                )
        for copy in copies:
            copy.start()
        for copy in copies:
            copy.wait()

    outs = pl.pallas_call(
        body,
        out_shape=[pltpu.VMEM((2, rows, width), keys.dtype)] * chips
        + [pltpu.VMEM((rows, width), values.dtype)] * chips,
        in_specs=[ANY] * 3,
        out_specs=in_vmem(2 * chips),
        scratch_shapes=[pltpu.SemaphoreType.DMA((3 * chips,))],
        name="pack",
    )(queries, keys, values)
    return outs[:chips], outs[chips:]


def join(blocks, slots, flops=0):
    chips, parts = len(blocks), blocks[0].shape[:-2]
    rows, width = blocks[0].shape[-2:]
    count = parts[0] if parts else 1

    def body(*refs):
        for slot, block in enumerate(refs[:chips]):
            for part, out in enumerate(refs[chips:]):
                out[chip_rows(flip_of(slots[(slot + 1) % chips]), rows), :] = block[part] if parts else block[...]

    return pl.pallas_call(
        body,
        out_shape=[pltpu.VMEM((chips * rows, width), blocks[0].dtype)] * count,
        in_specs=in_vmem(chips),
        out_specs=in_vmem(count),
        cost_estimate=pl.CostEstimate(flops=flops, bytes_accessed=0, transcendentals=0),
        name="join",
    )(*resident(*blocks[1:], blocks[0]))


def pair(first, second):
    def body(first_ref, second_ref, out_ref):
        out_ref[0] = first_ref[...]
        out_ref[1] = second_ref[...]

    return pl.pallas_call(
        body,
        out_shape=pltpu.VMEM((2, *first.shape), first.dtype),
        in_specs=in_vmem(2),
        out_specs=in_vmem(1)[0],
        name="pair",
    )(*resident(first, second))


def chip_rows(flip, rows):
    chip = lax.axis_index("sp") // CORES
    return pl.ds(pl.multiple_of((chip ^ flip) * rows, rows), rows)


def turn(x, bit):
    return lax.ppermute(x, "grp", [(i, i ^ (1 << bit)) for i in range(lax.axis_size("grp"))])


def choose(mine, theirs, anchor, bit, after=()):
    def body(anchor_ref, mine_ref, theirs_ref, *rest):
        out_ref = rest[-1]
        same = ((anchor_ref[0] % lax.axis_size("grp") ^ lax.axis_index("grp")) >> bit) & 1

        @pl.when(same == 0)
        def _():
            out_ref[...] = mine_ref[...]

        @pl.when(same != 0)
        def _():
            out_ref[...] = theirs_ref[...]

    return pl.pallas_call(
        body,
        out_shape=pltpu.VMEM(mine.shape, mine.dtype),
        in_specs=[SMEM] + in_vmem(2 + len(after)),
        out_specs=in_vmem(1)[0],
        name="choose",
    )(anchor, *resident(mine, theirs, *after))


def scores_of(q, k_ref, columns):
    return lax.dot_general(
        q, k_ref[:, columns], (((1,), (1,)), ((), ())), preferred_element_type=jnp.float32
    )


def mix(weights, v_ref, columns):
    return jnp.dot(weights, v_ref[:, columns], preferred_element_type=jnp.float32)


def each_chunk(length, chunk):
    step = min(256, length)
    if length == step:
        chunk(0, step)
    else:
        pl.loop(0, length // step)(lambda index: chunk(pl.multiple_of(index * step, step), step))


def cost(length, width):
    return pl.CostEstimate(
        flops=8 * length * length * width,
        bytes_accessed=0,
        transcendentals=2 * length * length * (width // HD),
    )


def weigh(q, own_k, other_k, columns, own_mask, other_mask, before=None):
    first = own_mask(scores_of(q, own_k, columns))
    second = other_mask(scores_of(q, other_k, columns))
    top = jnp.maximum(jnp.max(first, axis=1, keepdims=True), jnp.max(second, axis=1, keepdims=True))
    if before is not None:
        top = jnp.maximum(top, before)
    first = jnp.exp2((first - top) * EXP_SCALE)
    second = jnp.exp2((second - top) * EXP_SCALE)
    total = jnp.sum(first, axis=1, keepdims=True) + jnp.sum(second, axis=1, keepdims=True)
    return first.astype(jnp.bfloat16), second.astype(jnp.bfloat16), top, total


def near(q_rows, own_k, own_v, other, positions):
    length, width = q_rows.shape
    chips = lax.axis_size("sp") // CORES
    rows = length // chips
    paired = CORES * rows == HD and chips % 2 == 0
    if not paired:
        positions = jnp.swapaxes(positions.reshape(chips, CORES, rows), 0, 1).reshape(CORES, length)

    def split(at):
        if not paired:
            return [jnp.broadcast_to(at[c : c + 1, :], (8, length)) for c in range(CORES)]
        low = lax.broadcasted_iota(jnp.int32, (8, HD), 1) < rows
        tokens = [jnp.broadcast_to(at[:, c * HD : (c + 1) * HD], (8, HD)) for c in range(chips)]
        turned = [pltpu.roll(row, rows, 1) for row in tokens]
        pairs = range(0, chips, 2)
        return [
            jnp.concatenate([jnp.where(low, tokens[c], turned[c + 1]) for c in pairs], 1),
            jnp.concatenate([jnp.where(low, turned[c], tokens[c + 1]) for c in pairs], 1),
        ]

    def body(q_ref, own_k, own_v, other_kv, at, top_ref, sum_ref, acc_ref, end_ref, own_at):
        end_ref[...] = jnp.zeros_like(end_ref)
        other_k, other_v = other_kv.at[0], other_kv.at[1]
        core = lax.axis_index("sp") % CORES
        first_at, second_at = split(at)
        own_at[...] = jnp.where(core == 0, first_at, second_at)
        other_at = jnp.where(core == 0, second_at, first_at)[:1, :]

        def chunk(start, step):
            here = pl.ds(start, step)
            order = jnp.transpose(jnp.broadcast_to(own_at[:1, here], (HD, step)))[:, :1]
            for head in range(width // HD):
                columns = slice(head * HD, (head + 1) * HD)
                first, second, top, total = weigh(
                    q_ref[here, columns],
                    own_k,
                    other_k,
                    columns,
                    lambda scores: jnp.where(own_at[:1, :] <= order, scores, NEG),
                    lambda scores: jnp.where(other_at <= order, scores, NEG),
                )
                top_ref[head, here, :] = jnp.broadcast_to(top, (step, HD))
                sum_ref[head, here, :] = jnp.broadcast_to(total, (step, HD))
                acc_ref[here, columns] = mix(first, own_v, columns) + mix(second, other_v, columns)

        each_chunk(length, chunk)

    state = pltpu.VMEM((width // HD, length, HD), jnp.float32)
    return pl.pallas_call(
        body,
        out_shape=[
            state,
            state,
            pltpu.VMEM((length, width), jnp.float32),
            pltpu.VMEM((8, HD), jnp.float32),
        ],
        in_specs=in_vmem(5),
        out_specs=in_vmem(4),
        scratch_shapes=[pltpu.VMEM((8, length), jnp.int32)],
        compiler_params=pltpu.CompilerParams(vmem_limit_bytes=VMEM_LIMIT),
        cost_estimate=cost(length, width),
        name="near",
    )(*resident(q_rows, own_k, own_v, other), positions)


def far_weights(q_rows, top, own_k, other_k, anchor):
    length, width = q_rows.shape
    heads = width // HD

    def body(anchor_ref, q_ref, old_ref, own_k, other_k, first_ref, second_ref, top_ref, sum_ref):
        hidden = lax.axis_index("grp") == anchor_ref[0] % lax.axis_size("grp")

        def mask(scores):
            return jnp.where(hidden, NEG, scores)

        def chunk(start, step):
            here = pl.ds(start, step)
            for head in range(heads):
                columns = slice(head * HD, (head + 1) * HD)
                old = old_ref[head, here, :][:, :1]
                first, second, top, total = weigh(
                    q_ref[here, columns], own_k, other_k, columns, mask, mask, old
                )
                first_ref[head, here, :] = first
                second_ref[head, here, :] = second
                top_ref[head, here, :] = jnp.broadcast_to(top, (step, HD))
                sum_ref[head, here, :] = jnp.broadcast_to(total, (step, HD))

        each_chunk(length, chunk)

    weights = pltpu.VMEM((heads, length, length), jnp.bfloat16)
    state = pltpu.VMEM((heads, length, HD), jnp.float32)
    return pl.pallas_call(
        body,
        out_shape=[weights, weights, state, state],
        in_specs=[SMEM] + in_vmem(4),
        out_specs=in_vmem(4),
        compiler_params=pltpu.CompilerParams(vmem_limit_bytes=VMEM_LIMIT),
        cost_estimate=cost(length, width),
        name="far_weights",
    )(anchor, *resident(q_rows, top, own_k, other_k))


def far_values(near_state, far_state, own_v, other_v, slots):
    length, width = near_state[-1].shape
    chips = lax.axis_size("sp") // CORES
    rows = length // chips

    def body(*refs):
        old_top, old_sum, old_acc, first_ref, second_ref, top_ref, sum_ref, own_v, other_v = refs[:9]
        out_refs, done = refs[9:-1], refs[-1]

        def chunk(start, step):
            here = pl.ds(start, step)
            for head in range(width // HD):
                columns = slice(head * HD, (head + 1) * HD)
                keep = jnp.exp2((old_top[head, here, :] - top_ref[head, here, :]) * EXP_SCALE)
                total = keep * old_sum[head, here, :] + sum_ref[head, here, :]
                acc = (
                    keep * old_acc[here, columns]
                    + mix(first_ref[head, here, :], own_v, columns)
                    + mix(second_ref[head, here, :], other_v, columns)
                )
                done[here, columns] = (acc / total).astype(jnp.bfloat16)

        each_chunk(length, chunk)
        for slot, out in enumerate(out_refs):
            out[...] = done[chip_rows(flip_of(slots[slot]), rows), :]

    return pl.pallas_call(
        body,
        out_shape=[pltpu.VMEM((rows, width), jnp.bfloat16)] * chips,
        in_specs=in_vmem(9),
        out_specs=in_vmem(chips),
        scratch_shapes=[pltpu.VMEM((length, width), jnp.bfloat16)],
        compiler_params=pltpu.CompilerParams(vmem_limit_bytes=VMEM_LIMIT),
        cost_estimate=cost(length, width),
        name="far_values",
    )(*resident(*near_state, *far_state, own_v, other_v))


def unpack(blocks, slots):
    chips = len(blocks)
    rows, width = blocks[0].shape

    def body(*refs):
        block_refs, out_ref, sems = refs[:chips], refs[chips], refs[-1]
        chip = lax.axis_index("sp") // CORES
        copies = []
        for slot, block in enumerate(block_refs):
            flip = flip_of(slots[(slot + 1) % chips])
            columns = pl.ds(pl.multiple_of((chip ^ flip) * width, HD), width)
            copies.append(pltpu.make_async_copy(block, out_ref.at[0, :, columns], sems.at[slot]))
        for copy in copies:
            copy.start()
        for copy in copies:
            copy.wait()

    return pl.pallas_call(
        body,
        out_shape=jax.ShapeDtypeStruct((1, rows, chips * width), blocks[0].dtype),
        in_specs=in_vmem(chips),
        out_specs=ANY,
        scratch_shapes=[pltpu.SemaphoreType.DMA((chips,))],
        name="unpack",
    )(*resident(*blocks[1:], blocks[0]))


def trade(blocks, slots):
    devices = lax.axis_size("sp")
    moved = [
        lax.ppermute(block, "sp", [(i, i ^ (CORES * flips[i % CORES])) for i in range(devices)])
        for block, flips in zip(blocks[1:], slots[1:])
    ]
    return [blocks[0], *moved]


def on_device(queries, keys, values, positions, anchor):
    chips = lax.axis_size("sp") // CORES
    distant_first = [*reversed(range(1, chips))]
    crossing_first = sorted(distant_first, key=lambda flip: (flip < chips // 2, flip))
    nearest_first = [1, *distant_first[:-1]] if chips > 1 else []
    kv_slots = [(0, 0), *zip(crossing_first, distant_first)]
    q_slots = [(0, 0), *zip(distant_first, nearest_first)]
    out_slots = [(0, 0), *zip(distant_first, distant_first)]

    kv_blocks, q_blocks = pack(queries, keys, values, kv_slots, q_slots)
    k_own, v_own = join(trade(kv_blocks, kv_slots), kv_slots)
    (q_rows,) = join(trade(q_blocks, q_slots), q_slots, QUERY_FLOPS)
    other = swap(pair(k_own, v_own), 1)

    bits = lax.axis_size("grp").bit_length() - 1
    k_far, v_far, *state, end = k_own, v_own, *near(q_rows, k_own, v_own, other, positions)
    for stage in range(bits):
        after = [[q_rows], [end]][stage] if stage < 2 else ()
        back = bits - 1 - stage
        k_far = choose(k_far, turn(k_far, stage), anchor, stage, after)
        v_far = choose(v_far, turn(v_far, back), anchor, back)
    far_state = far_weights(q_rows, state[0], k_far, swap(k_far, 1), anchor)
    done = far_values(state, far_state, v_far, swap(v_far, 1), out_slots)
    return unpack(trade(done, out_slots), out_slots)


def solution(mesh):
    return jax.shard_map(
        on_device,
        mesh=mesh,
        in_specs=(
            P("grp", "sp", None),
            P("grp", "sp", None),
            P("grp", "sp", None),
            P("grp", None),
            P(),
        ),
        out_specs=P("grp", "sp", None),
        check_vma=False,
    )
```

```python
import math

import jax
import jax.numpy as jnp
from jax import lax
from jax.experimental import pallas as pl
from jax.experimental.pallas import tpu as pltpu
from jax.sharding import PartitionSpec as P

HD = 128
CORES = 2
NEG = -1e30
EXP_SCALE = 1.0 / (math.sqrt(HD) * math.log(2.0))
VMEM_LIMIT = 48 * 2**20
QUERY_FLOPS = 10**10
ANY = pl.BlockSpec(memory_space=pl.ANY)
SMEM = pl.BlockSpec(memory_space=pltpu.SMEM)


def in_vmem(count):
    return [pl.BlockSpec(memory_space=pltpu.VMEM)] * count


def resident(*arrays):
    return [pltpu.with_memory_space_constraint(x, pltpu.VMEM) for x in arrays]


def swap(x, flip):
    return lax.ppermute(x, "sp", [(i, i ^ flip) for i in range(lax.axis_size("sp"))])


def flip_of(flips):
    return jnp.where(lax.axis_index("sp") % CORES == 0, flips[0], flips[1])


def pack(queries, keys, values, kv_slots, q_slots):
    chips = lax.axis_size("sp") // CORES
    rows, width = queries.shape[1], queries.shape[2] // chips

    def body(q_ref, k_ref, v_ref, *rest):
        kv_refs, q_refs, sems = rest[:chips], rest[chips : 2 * chips], rest[-1]
        chip = lax.axis_index("sp") // CORES
        copies = []
        for slot in reversed(range(chips)):
            targets = (kv_refs[slot].at[0], kv_refs[slot].at[1], q_refs[slot])
            for part, source in enumerate((k_ref, v_ref, q_ref)):
                flip = flip_of((q_slots if part == 2 else kv_slots)[slot])
                columns = pl.ds(pl.multiple_of((chip ^ flip) * width, HD), width)
                copies.append(
                    pltpu.make_async_copy(
                        source.at[0, :, columns], targets[part], sems.at[3 * slot + part]
                    )
                )
        for copy in copies:
            copy.start()
        for copy in copies:
            copy.wait()

    outs = pl.pallas_call(
        body,
        out_shape=[pltpu.VMEM((2, rows, width), keys.dtype)] * chips
        + [pltpu.VMEM((rows, width), values.dtype)] * chips,
        in_specs=[ANY] * 3,
        out_specs=in_vmem(2 * chips),
        scratch_shapes=[pltpu.SemaphoreType.DMA((3 * chips,))],
        name="pack",
    )(queries, keys, values)
    return outs[:chips], outs[chips:]


def join(blocks, slots, flops=0):
    chips, parts = len(blocks), blocks[0].shape[:-2]
    rows, width = blocks[0].shape[-2:]
    count = parts[0] if parts else 1

    def body(*refs):
        for slot, block in enumerate(refs[:chips]):
            for part, out in enumerate(refs[chips:]):
                out[chip_rows(flip_of(slots[(slot + 1) % chips]), rows), :] = block[part] if parts else block[...]

    return pl.pallas_call(
        body,
        out_shape=[pltpu.VMEM((chips * rows, width), blocks[0].dtype)] * count,
        in_specs=in_vmem(chips),
        out_specs=in_vmem(count),
        cost_estimate=pl.CostEstimate(flops=flops, bytes_accessed=0, transcendentals=0),
        name="join",
    )(*resident(*blocks[1:], blocks[0]))


def hold(blocks, after=(), flops=0):
    count = len(blocks)

    def body(*refs):
        for source, target in zip(refs[:count], refs[count + len(after) : -1]):
            target[...] = source[...]
        refs[-1][...] = jnp.zeros_like(refs[-1])

    return pl.pallas_call(
        body,
        out_shape=[pltpu.VMEM(block.shape, block.dtype) for block in blocks] + [pltpu.VMEM((8, HD), jnp.float32)],
        in_specs=in_vmem(count + len(after)),
        out_specs=in_vmem(count + 1),
        cost_estimate=pl.CostEstimate(flops=flops, bytes_accessed=0, transcendentals=0),
        name="hold",
    )(*resident(*blocks, *after))


def pair(first, second):
    def body(first_ref, second_ref, out_ref):
        out_ref[0] = first_ref[...]
        out_ref[1] = second_ref[...]

    return pl.pallas_call(
        body,
        out_shape=pltpu.VMEM((2, *first.shape), first.dtype),
        in_specs=in_vmem(2),
        out_specs=in_vmem(1)[0],
        name="pair",
    )(*resident(first, second))


def chip_rows(flip, rows):
    chip = lax.axis_index("sp") // CORES
    return pl.ds(pl.multiple_of((chip ^ flip) * rows, rows), rows)


def turn(x, bit):
    return lax.ppermute(x, "grp", [(i, i ^ (1 << bit)) for i in range(lax.axis_size("grp"))])


def choose(mine, theirs, anchor, bit, after=()):
    def body(anchor_ref, mine_ref, theirs_ref, *rest):
        out_ref = rest[-1]
        same = ((anchor_ref[0] % lax.axis_size("grp") ^ lax.axis_index("grp")) >> bit) & 1

        @pl.when(same == 0)
        def _():
            out_ref[...] = mine_ref[...]

        @pl.when(same != 0)
        def _():
            out_ref[...] = theirs_ref[...]

    return pl.pallas_call(
        body,
        out_shape=pltpu.VMEM(mine.shape, mine.dtype),
        in_specs=[SMEM] + in_vmem(2 + len(after)),
        out_specs=in_vmem(1)[0],
        name="choose",
    )(anchor, *resident(mine, theirs, *after))


def scores_of(q, k_ref, columns):
    return lax.dot_general(
        q, k_ref[:, columns], (((1,), (1,)), ((), ())), preferred_element_type=jnp.float32
    )


def mix(weights, v_ref, columns):
    return jnp.dot(weights, v_ref[:, columns], preferred_element_type=jnp.float32)


def each_chunk(length, chunk):
    step = min(256, length)
    if length == step:
        chunk(0, step)
    else:
        pl.loop(0, length // step)(lambda index: chunk(pl.multiple_of(index * step, step), step))


def cost(length, width):
    return pl.CostEstimate(
        flops=8 * length * length * width,
        bytes_accessed=0,
        transcendentals=2 * length * length * (width // HD),
    )


def weigh(q, own_k, other_k, columns, own_mask, other_mask, before=None):
    first = own_mask(scores_of(q, own_k, columns))
    second = other_mask(scores_of(q, other_k, columns))
    top = jnp.maximum(jnp.max(first, axis=1, keepdims=True), jnp.max(second, axis=1, keepdims=True))
    if before is not None:
        top = jnp.maximum(top, before)
    first = jnp.exp2((first - top) * EXP_SCALE)
    second = jnp.exp2((second - top) * EXP_SCALE)
    total = jnp.sum(first, axis=1, keepdims=True) + jnp.sum(second, axis=1, keepdims=True)
    return first.astype(jnp.bfloat16), second.astype(jnp.bfloat16), top, total


def near(q_rows, own_k, own_v, other, positions):
    length, width = q_rows.shape
    chips = lax.axis_size("sp") // CORES
    rows = length // chips
    paired = CORES * rows == HD and chips % 2 == 0
    if not paired:
        positions = jnp.swapaxes(positions.reshape(chips, CORES, rows), 0, 1).reshape(CORES, length)

    def split(at):
        if not paired:
            return [jnp.broadcast_to(at[c : c + 1, :], (8, length)) for c in range(CORES)]
        low = lax.broadcasted_iota(jnp.int32, (8, HD), 1) < rows
        tokens = [jnp.broadcast_to(at[:, c * HD : (c + 1) * HD], (8, HD)) for c in range(chips)]
        turned = [pltpu.roll(row, rows, 1) for row in tokens]
        pairs = range(0, chips, 2)
        return [
            jnp.concatenate([jnp.where(low, tokens[c], turned[c + 1]) for c in pairs], 1),
            jnp.concatenate([jnp.where(low, turned[c], tokens[c + 1]) for c in pairs], 1),
        ]

    def body(q_ref, own_k, own_v, other_kv, at, top_ref, sum_ref, acc_ref, end_ref, own_at):
        end_ref[...] = jnp.zeros_like(end_ref)
        other_k, other_v = other_kv.at[0], other_kv.at[1]
        core = lax.axis_index("sp") % CORES
        first_at, second_at = split(at)
        own_at[...] = jnp.where(core == 0, first_at, second_at)
        other_at = jnp.where(core == 0, second_at, first_at)[:1, :]

        def chunk(start, step):
            here = pl.ds(start, step)
            order = jnp.transpose(jnp.broadcast_to(own_at[:1, here], (HD, step)))[:, :1]
            for head in range(width // HD):
                columns = slice(head * HD, (head + 1) * HD)
                first, second, top, total = weigh(
                    q_ref[here, columns],
                    own_k,
                    other_k,
                    columns,
                    lambda scores: jnp.where(own_at[:1, :] <= order, scores, NEG),
                    lambda scores: jnp.where(other_at <= order, scores, NEG),
                )
                top_ref[head, here, :] = jnp.broadcast_to(top, (step, HD))
                sum_ref[head, here, :] = jnp.broadcast_to(total, (step, HD))
                acc_ref[here, columns] = mix(first, own_v, columns) + mix(second, other_v, columns)

        each_chunk(length, chunk)

    state = pltpu.VMEM((width // HD, length, HD), jnp.float32)
    return pl.pallas_call(
        body,
        out_shape=[
            state,
            state,
            pltpu.VMEM((length, width), jnp.float32),
            pltpu.VMEM((8, HD), jnp.float32),
        ],
        in_specs=in_vmem(5),
        out_specs=in_vmem(4),
        scratch_shapes=[pltpu.VMEM((8, length), jnp.int32)],
        compiler_params=pltpu.CompilerParams(vmem_limit_bytes=VMEM_LIMIT),
        cost_estimate=cost(length, width),
        name="near",
    )(*resident(q_rows, own_k, own_v, other), positions)


def far_weights(q_rows, top, own_k, other_k, anchor):
    length, width = q_rows.shape
    heads = width // HD

    def body(anchor_ref, q_ref, old_ref, own_k, other_k, first_ref, second_ref, top_ref, sum_ref):
        hidden = lax.axis_index("grp") == anchor_ref[0] % lax.axis_size("grp")

        def mask(scores):
            return jnp.where(hidden, NEG, scores)

        def chunk(start, step):
            here = pl.ds(start, step)
            for head in range(heads):
                columns = slice(head * HD, (head + 1) * HD)
                old = old_ref[head, here, :][:, :1]
                first, second, top, total = weigh(
                    q_ref[here, columns], own_k, other_k, columns, mask, mask, old
                )
                first_ref[head, here, :] = first
                second_ref[head, here, :] = second
                top_ref[head, here, :] = jnp.broadcast_to(top, (step, HD))
                sum_ref[head, here, :] = jnp.broadcast_to(total, (step, HD))

        each_chunk(length, chunk)

    weights = pltpu.VMEM((heads, length, length), jnp.bfloat16)
    state = pltpu.VMEM((heads, length, HD), jnp.float32)
    return pl.pallas_call(
        body,
        out_shape=[weights, weights, state, state],
        in_specs=[SMEM] + in_vmem(4),
        out_specs=in_vmem(4),
        compiler_params=pltpu.CompilerParams(vmem_limit_bytes=VMEM_LIMIT),
        cost_estimate=cost(length, width),
        name="far_weights",
    )(anchor, *resident(q_rows, top, own_k, other_k))


def far_values(near_state, far_state, own_v, other_v, slots):
    length, width = near_state[-1].shape
    chips = lax.axis_size("sp") // CORES
    rows = length // chips

    def body(*refs):
        old_top, old_sum, old_acc, first_ref, second_ref, top_ref, sum_ref, own_v, other_v = refs[:9]
        out_refs, done = refs[9:-1], refs[-1]

        def chunk(start, step):
            here = pl.ds(start, step)
            for head in range(width // HD):
                columns = slice(head * HD, (head + 1) * HD)
                keep = jnp.exp2((old_top[head, here, :] - top_ref[head, here, :]) * EXP_SCALE)
                total = keep * old_sum[head, here, :] + sum_ref[head, here, :]
                acc = (
                    keep * old_acc[here, columns]
                    + mix(first_ref[head, here, :], own_v, columns)
                    + mix(second_ref[head, here, :], other_v, columns)
                )
                done[here, columns] = (acc / total).astype(jnp.bfloat16)

        each_chunk(length, chunk)
        for slot, out in enumerate(out_refs):
            out[...] = done[chip_rows(flip_of(slots[slot]), rows), :]

    return pl.pallas_call(
        body,
        out_shape=[pltpu.VMEM((rows, width), jnp.bfloat16)] * chips,
        in_specs=in_vmem(9),
        out_specs=in_vmem(chips),
        scratch_shapes=[pltpu.VMEM((length, width), jnp.bfloat16)],
        compiler_params=pltpu.CompilerParams(vmem_limit_bytes=VMEM_LIMIT),
        cost_estimate=cost(length, width),
        name="far_values",
    )(*resident(*near_state, *far_state, own_v, other_v))


def unpack(blocks, slots):
    chips = len(blocks)
    rows, width = blocks[0].shape

    def body(*refs):
        block_refs, out_ref, sems = refs[:chips], refs[chips], refs[-1]
        chip = lax.axis_index("sp") // CORES
        copies = []
        for slot, block in enumerate(block_refs):
            flip = flip_of(slots[(slot + 1) % chips])
            columns = pl.ds(pl.multiple_of((chip ^ flip) * width, HD), width)
            copies.append(pltpu.make_async_copy(block, out_ref.at[0, :, columns], sems.at[slot]))
        for copy in copies:
            copy.start()
        for copy in copies:
            copy.wait()

    return pl.pallas_call(
        body,
        out_shape=jax.ShapeDtypeStruct((1, rows, chips * width), blocks[0].dtype),
        in_specs=in_vmem(chips),
        out_specs=ANY,
        scratch_shapes=[pltpu.SemaphoreType.DMA((chips,))],
        name="unpack",
    )(*resident(*blocks[1:], blocks[0]))


def trade(blocks, slots):
    devices = lax.axis_size("sp")
    moved = [
        lax.ppermute(block, "sp", [(i, i ^ (CORES * flips[i % CORES])) for i in range(devices)])
        for block, flips in zip(blocks[1:], slots[1:])
    ]
    return [blocks[0], *moved]


def on_device(queries, keys, values, positions, anchor):
    chips = lax.axis_size("sp") // CORES
    distant_first = [*reversed(range(1, chips))]
    crossing_first = sorted(distant_first, key=lambda flip: (flip < chips // 2, flip))
    kv_slots = [(0, 0), *zip(crossing_first, distant_first)]
    q_slots = [(0, 0), *zip(distant_first, distant_first)]
    out_slots = [(0, 0), *zip(distant_first, distant_first)]

    kv_blocks, q_blocks = pack(queries, keys, values, kv_slots, q_slots)
    moved = trade([q_blocks[0], q_blocks[-1]], [q_slots[0], q_slots[-1]])
    nearest, _ = hold(moved[1:], flops=QUERY_FLOPS)
    moved = [moved[0], nearest]
    k_own, v_own = join(trade(kv_blocks, kv_slots), kv_slots)
    other = swap(pair(k_own, v_own), 1)
    *distant, seen = hold(trade(q_blocks[:-1], q_slots[:-1])[1:], flops=QUERY_FLOPS)
    (q_rows,) = join([*moved[:1], *distant, *moved[1:]], q_slots)

    bits = lax.axis_size("grp").bit_length() - 1
    k_far, v_far, *state, end = k_own, v_own, *near(q_rows, k_own, v_own, other, positions)
    for stage in range(bits):
        after = [[seen], [end]][stage] if stage < 2 else ()
        back = bits - 1 - stage
        k_far = choose(k_far, turn(k_far, stage), anchor, stage, after)
        v_far = choose(v_far, turn(v_far, back), anchor, back)
    far_state = far_weights(q_rows, state[0], k_far, swap(k_far, 1), anchor)
    done = far_values(state, far_state, v_far, swap(v_far, 1), out_slots)
    return unpack(trade(done, out_slots), out_slots)


def solution(mesh):
    return jax.shard_map(
        on_device,
        mesh=mesh,
        in_specs=(
            P("grp", "sp", None),
            P("grp", "sp", None),
            P("grp", "sp", None),
            P("grp", None),
            P(),
        ),
        out_specs=P("grp", "sp", None),
        check_vma=False,
    )
```

```python
import math

import jax
import jax.numpy as jnp
from jax import lax
from jax.experimental import pallas as pl
from jax.experimental.pallas import tpu as pltpu
from jax.sharding import PartitionSpec as P

HD = 128
CORES = 2
NEG = -1e30
EXP_SCALE = 1.0 / (math.sqrt(HD) * math.log(2.0))
VMEM_LIMIT = 48 * 2**20
QUERY_FLOPS = 10**10
ANY = pl.BlockSpec(memory_space=pl.ANY)
SMEM = pl.BlockSpec(memory_space=pltpu.SMEM)


def in_vmem(count):
    return [pl.BlockSpec(memory_space=pltpu.VMEM)] * count


def resident(*arrays):
    return [pltpu.with_memory_space_constraint(x, pltpu.VMEM) for x in arrays]


def swap(x, flip):
    return lax.ppermute(x, "sp", [(i, i ^ flip) for i in range(lax.axis_size("sp"))])


def flip_of(flips):
    return jnp.where(lax.axis_index("sp") % CORES == 0, flips[0], flips[1])


def pack(queries, keys, values, kv_slots, q_slots):
    chips = lax.axis_size("sp") // CORES
    rows, width = queries.shape[1], queries.shape[2] // chips

    def body(q_ref, k_ref, v_ref, *rest):
        kv_refs, q_refs, sems = rest[:chips], rest[chips : 2 * chips], rest[-1]
        chip = lax.axis_index("sp") // CORES
        copies = []
        for slot in reversed(range(chips)):
            targets = (kv_refs[slot].at[0], kv_refs[slot].at[1], q_refs[slot])
            for part, source in enumerate((k_ref, v_ref, q_ref)):
                flip = flip_of((q_slots if part == 2 else kv_slots)[slot])
                columns = pl.ds(pl.multiple_of((chip ^ flip) * width, HD), width)
                copies.append(
                    pltpu.make_async_copy(
                        source.at[0, :, columns], targets[part], sems.at[3 * slot + part]
                    )
                )
        for copy in copies:
            copy.start()
        for copy in copies:
            copy.wait()

    outs = pl.pallas_call(
        body,
        out_shape=[pltpu.VMEM((2, rows, width), keys.dtype)] * chips
        + [pltpu.VMEM((rows, width), values.dtype)] * chips,
        in_specs=[ANY] * 3,
        out_specs=in_vmem(2 * chips),
        scratch_shapes=[pltpu.SemaphoreType.DMA((3 * chips,))],
        name="pack",
    )(queries, keys, values)
    return outs[:chips], outs[chips:]


def join(blocks, slots, flops=0):
    chips, parts = len(blocks), blocks[0].shape[:-2]
    rows, width = blocks[0].shape[-2:]
    count = parts[0] if parts else 1

    def body(*refs):
        for slot, block in enumerate(refs[:chips]):
            for part, out in enumerate(refs[chips:]):
                out[chip_rows(flip_of(slots[(slot + 1) % chips]), rows), :] = block[part] if parts else block[...]

    return pl.pallas_call(
        body,
        out_shape=[pltpu.VMEM((chips * rows, width), blocks[0].dtype)] * count,
        in_specs=in_vmem(chips),
        out_specs=in_vmem(count),
        cost_estimate=pl.CostEstimate(flops=flops, bytes_accessed=0, transcendentals=0),
        name="join",
    )(*resident(*blocks[1:], blocks[0]))


def hold(blocks, after=(), flops=0):
    count = len(blocks)

    def body(*refs):
        for source, target in zip(refs[:count], refs[count + len(after) : -1]):
            target[...] = source[...]
        refs[-1][...] = jnp.zeros_like(refs[-1])

    return pl.pallas_call(
        body,
        out_shape=[pltpu.VMEM(block.shape, block.dtype) for block in blocks] + [pltpu.VMEM((8, HD), jnp.float32)],
        in_specs=in_vmem(count + len(after)),
        out_specs=in_vmem(count + 1),
        cost_estimate=pl.CostEstimate(flops=flops, bytes_accessed=0, transcendentals=0),
        name="hold",
    )(*resident(*blocks, *after))


def pair(first, second):
    def body(first_ref, second_ref, out_ref):
        out_ref[0] = first_ref[...]
        out_ref[1] = second_ref[...]

    return pl.pallas_call(
        body,
        out_shape=pltpu.VMEM((2, *first.shape), first.dtype),
        in_specs=in_vmem(2),
        out_specs=in_vmem(1)[0],
        name="pair",
    )(*resident(first, second))


def chip_rows(flip, rows):
    chip = lax.axis_index("sp") // CORES
    return pl.ds(pl.multiple_of((chip ^ flip) * rows, rows), rows)


def turn(x, bit):
    return lax.ppermute(x, "grp", [(i, i ^ (1 << bit)) for i in range(lax.axis_size("grp"))])


def choose(mine, theirs, anchor, bit, after=()):
    def body(anchor_ref, mine_ref, theirs_ref, *rest):
        out_ref = rest[-1]
        same = ((anchor_ref[0] % lax.axis_size("grp") ^ lax.axis_index("grp")) >> bit) & 1

        @pl.when(same == 0)
        def _():
            out_ref[...] = mine_ref[...]

        @pl.when(same != 0)
        def _():
            out_ref[...] = theirs_ref[...]

    return pl.pallas_call(
        body,
        out_shape=pltpu.VMEM(mine.shape, mine.dtype),
        in_specs=[SMEM] + in_vmem(2 + len(after)),
        out_specs=in_vmem(1)[0],
        name="choose",
    )(anchor, *resident(mine, theirs, *after))


def scores_of(q, k_ref, columns):
    return lax.dot_general(
        q, k_ref[:, columns], (((1,), (1,)), ((), ())), preferred_element_type=jnp.float32
    )


def mix(weights, v_ref, columns):
    return jnp.dot(weights, v_ref[:, columns], preferred_element_type=jnp.float32)


def each_chunk(length, chunk):
    step = min(256, length)
    if length == step:
        chunk(0, step)
    else:
        pl.loop(0, length // step)(lambda index: chunk(pl.multiple_of(index * step, step), step))


def cost(length, width):
    return pl.CostEstimate(
        flops=8 * length * length * width,
        bytes_accessed=0,
        transcendentals=2 * length * length * (width // HD),
    )


def weigh(q, own_k, other_k, columns, own_mask, other_mask, before=None):
    first = own_mask(scores_of(q, own_k, columns))
    second = other_mask(scores_of(q, other_k, columns))
    top = jnp.maximum(jnp.max(first, axis=1, keepdims=True), jnp.max(second, axis=1, keepdims=True))
    if before is not None:
        top = jnp.maximum(top, before)
    first = jnp.exp2((first - top) * EXP_SCALE)
    second = jnp.exp2((second - top) * EXP_SCALE)
    total = jnp.sum(first, axis=1, keepdims=True) + jnp.sum(second, axis=1, keepdims=True)
    return first.astype(jnp.bfloat16), second.astype(jnp.bfloat16), top, total


def near(q_rows, own_k, own_v, other, positions):
    length, width = q_rows.shape
    chips = lax.axis_size("sp") // CORES
    rows = length // chips
    paired = CORES * rows == HD and chips % 2 == 0
    if not paired:
        positions = jnp.swapaxes(positions.reshape(chips, CORES, rows), 0, 1).reshape(CORES, length)

    def split(at):
        if not paired:
            return [jnp.broadcast_to(at[c : c + 1, :], (8, length)) for c in range(CORES)]
        low = lax.broadcasted_iota(jnp.int32, (8, HD), 1) < rows
        tokens = [jnp.broadcast_to(at[:, c * HD : (c + 1) * HD], (8, HD)) for c in range(chips)]
        turned = [pltpu.roll(row, rows, 1) for row in tokens]
        pairs = range(0, chips, 2)
        return [
            jnp.concatenate([jnp.where(low, tokens[c], turned[c + 1]) for c in pairs], 1),
            jnp.concatenate([jnp.where(low, turned[c], tokens[c + 1]) for c in pairs], 1),
        ]

    def body(q_ref, own_k, own_v, other_kv, at, top_ref, sum_ref, acc_ref, end_ref, own_at):
        end_ref[...] = jnp.zeros_like(end_ref)
        other_k, other_v = other_kv.at[0], other_kv.at[1]
        core = lax.axis_index("sp") % CORES
        first_at, second_at = split(at)
        own_at[...] = jnp.where(core == 0, first_at, second_at)
        other_at = jnp.where(core == 0, second_at, first_at)[:1, :]

        def chunk(start, step):
            here = pl.ds(start, step)
            order = jnp.transpose(jnp.broadcast_to(own_at[:1, here], (HD, step)))[:, :1]
            for head in range(width // HD):
                columns = slice(head * HD, (head + 1) * HD)
                first, second, top, total = weigh(
                    q_ref[here, columns],
                    own_k,
                    other_k,
                    columns,
                    lambda scores: jnp.where(own_at[:1, :] <= order, scores, NEG),
                    lambda scores: jnp.where(other_at <= order, scores, NEG),
                )
                top_ref[head, here, :] = jnp.broadcast_to(top, (step, HD))
                sum_ref[head, here, :] = jnp.broadcast_to(total, (step, HD))
                acc_ref[here, columns] = mix(first, own_v, columns) + mix(second, other_v, columns)

        each_chunk(length, chunk)

    state = pltpu.VMEM((width // HD, length, HD), jnp.float32)
    return pl.pallas_call(
        body,
        out_shape=[
            state,
            state,
            pltpu.VMEM((length, width), jnp.float32),
            pltpu.VMEM((8, HD), jnp.float32),
        ],
        in_specs=in_vmem(5),
        out_specs=in_vmem(4),
        scratch_shapes=[pltpu.VMEM((8, length), jnp.int32)],
        compiler_params=pltpu.CompilerParams(vmem_limit_bytes=VMEM_LIMIT),
        cost_estimate=cost(length, width),
        name="near",
    )(*resident(q_rows, own_k, own_v, other), positions)


def far_weights(q_rows, top, own_k, other_k, anchor):
    length, width = q_rows.shape
    heads = width // HD

    def body(anchor_ref, q_ref, old_ref, own_k, other_k, first_ref, second_ref, top_ref, sum_ref):
        hidden = lax.axis_index("grp") == anchor_ref[0] % lax.axis_size("grp")

        def mask(scores):
            return jnp.where(hidden, NEG, scores)

        def chunk(start, step):
            here = pl.ds(start, step)
            for head in range(heads):
                columns = slice(head * HD, (head + 1) * HD)
                old = old_ref[head, here, :][:, :1]
                first, second, top, total = weigh(
                    q_ref[here, columns], own_k, other_k, columns, mask, mask, old
                )
                first_ref[head, here, :] = first
                second_ref[head, here, :] = second
                top_ref[head, here, :] = jnp.broadcast_to(top, (step, HD))
                sum_ref[head, here, :] = jnp.broadcast_to(total, (step, HD))

        each_chunk(length, chunk)

    weights = pltpu.VMEM((heads, length, length), jnp.bfloat16)
    state = pltpu.VMEM((heads, length, HD), jnp.float32)
    return pl.pallas_call(
        body,
        out_shape=[weights, weights, state, state],
        in_specs=[SMEM] + in_vmem(4),
        out_specs=in_vmem(4),
        compiler_params=pltpu.CompilerParams(vmem_limit_bytes=VMEM_LIMIT),
        cost_estimate=cost(length, width),
        name="far_weights",
    )(anchor, *resident(q_rows, top, own_k, other_k))


def far_values(near_state, far_state, own_v, other_v, slots):
    length, width = near_state[-1].shape
    chips = lax.axis_size("sp") // CORES
    rows = length // chips

    def body(*refs):
        old_top, old_sum, old_acc, first_ref, second_ref, top_ref, sum_ref, own_v, other_v = refs[:9]
        out_refs, done = refs[9:-1], refs[-1]

        def chunk(start, step):
            here = pl.ds(start, step)
            for head in range(width // HD):
                columns = slice(head * HD, (head + 1) * HD)
                keep = jnp.exp2((old_top[head, here, :] - top_ref[head, here, :]) * EXP_SCALE)
                total = keep * old_sum[head, here, :] + sum_ref[head, here, :]
                acc = (
                    keep * old_acc[here, columns]
                    + mix(first_ref[head, here, :], own_v, columns)
                    + mix(second_ref[head, here, :], other_v, columns)
                )
                done[here, columns] = (acc / total).astype(jnp.bfloat16)

        each_chunk(length, chunk)
        for slot, out in enumerate(out_refs):
            out[...] = done[chip_rows(flip_of(slots[slot]), rows), :]

    return pl.pallas_call(
        body,
        out_shape=[pltpu.VMEM((rows, width), jnp.bfloat16)] * chips,
        in_specs=in_vmem(9),
        out_specs=in_vmem(chips),
        scratch_shapes=[pltpu.VMEM((length, width), jnp.bfloat16)],
        compiler_params=pltpu.CompilerParams(vmem_limit_bytes=VMEM_LIMIT),
        cost_estimate=cost(length, width),
        name="far_values",
    )(*resident(*near_state, *far_state, own_v, other_v))


def unpack(blocks, slots):
    chips = len(blocks)
    rows, width = blocks[0].shape

    def body(*refs):
        block_refs, out_ref, sems = refs[:chips], refs[chips], refs[-1]
        chip = lax.axis_index("sp") // CORES
        copies = []
        for slot, block in enumerate(block_refs):
            flip = flip_of(slots[(slot + 1) % chips])
            columns = pl.ds(pl.multiple_of((chip ^ flip) * width, HD), width)
            copies.append(pltpu.make_async_copy(block, out_ref.at[0, :, columns], sems.at[slot]))
        for copy in copies:
            copy.start()
        for copy in copies:
            copy.wait()

    return pl.pallas_call(
        body,
        out_shape=jax.ShapeDtypeStruct((1, rows, chips * width), blocks[0].dtype),
        in_specs=in_vmem(chips),
        out_specs=ANY,
        scratch_shapes=[pltpu.SemaphoreType.DMA((chips,))],
        name="unpack",
    )(*resident(*blocks[1:], blocks[0]))


def trade(blocks, slots):
    devices = lax.axis_size("sp")
    moved = [
        lax.ppermute(block, "sp", [(i, i ^ (CORES * flips[i % CORES])) for i in range(devices)])
        for block, flips in zip(blocks[1:], slots[1:])
    ]
    return [blocks[0], *moved]


def on_device(queries, keys, values, positions, anchor):
    chips = lax.axis_size("sp") // CORES
    distant_first = [*reversed(range(1, chips))]
    crossing_first = sorted(distant_first, key=lambda flip: (flip < chips // 2, flip))
    kv_slots = [(0, 0), *zip(crossing_first, distant_first)]
    q_slots = [(0, 0), *zip(crossing_first, crossing_first)]
    out_slots = [(0, 0), *zip(distant_first, distant_first)]

    kv_blocks, q_blocks = pack(queries, keys, values, kv_slots, q_slots)
    moved = trade([q_blocks[0], q_blocks[-1]], [q_slots[0], q_slots[-1]])
    nearest, _ = hold(moved[1:], flops=QUERY_FLOPS)
    moved = [moved[0], nearest]
    k_own, v_own = join(trade(kv_blocks, kv_slots), kv_slots)
    other = swap(pair(k_own, v_own), 1)
    *distant, seen = hold(trade(q_blocks[:-1], q_slots[:-1])[1:], flops=QUERY_FLOPS)
    (q_rows,) = join([*moved[:1], *distant, *moved[1:]], q_slots)

    bits = lax.axis_size("grp").bit_length() - 1
    k_far, v_far, *state, end = k_own, v_own, *near(q_rows, k_own, v_own, other, positions)
    for stage in range(bits):
        after = [[seen], [end]][stage] if stage < 2 else ()
        back = bits - 1 - stage
        k_far = choose(k_far, turn(k_far, stage), anchor, stage, after)
        v_far = choose(v_far, turn(v_far, back), anchor, back)
    far_state = far_weights(q_rows, state[0], k_far, swap(k_far, 1), anchor)
    done = far_values(state, far_state, v_far, swap(v_far, 1), out_slots)
    return unpack(trade(done, out_slots), out_slots)


def solution(mesh):
    return jax.shard_map(
        on_device,
        mesh=mesh,
        in_specs=(
            P("grp", "sp", None),
            P("grp", "sp", None),
            P("grp", "sp", None),
            P("grp", None),
            P(),
        ),
        out_specs=P("grp", "sp", None),
        check_vma=False,
    )
```

```python
import math

import jax
import jax.numpy as jnp
from jax import lax
from jax.experimental import pallas as pl
from jax.experimental.pallas import tpu as pltpu
from jax.sharding import PartitionSpec as P

HD = 128
CORES = 2
NEG = -1e30
EXP_SCALE = 1.0 / (math.sqrt(HD) * math.log(2.0))
VMEM_LIMIT = 48 * 2**20
QUERY_FLOPS = 10**10
ANY = pl.BlockSpec(memory_space=pl.ANY)
SMEM = pl.BlockSpec(memory_space=pltpu.SMEM)


def in_vmem(count):
    return [pl.BlockSpec(memory_space=pltpu.VMEM)] * count


def resident(*arrays):
    return [pltpu.with_memory_space_constraint(x, pltpu.VMEM) for x in arrays]


def swap(x, flip):
    return lax.ppermute(x, "sp", [(i, i ^ flip) for i in range(lax.axis_size("sp"))])


def flip_of(flips):
    return jnp.where(lax.axis_index("sp") % CORES == 0, flips[0], flips[1])


def pack(queries, keys, values, kv_slots, q_slots):
    chips = lax.axis_size("sp") // CORES
    rows, width = queries.shape[1], queries.shape[2] // chips

    def body(q_ref, k_ref, v_ref, *rest):
        kv_refs, q_refs, sems = rest[:chips], rest[chips : 2 * chips], rest[-1]
        chip = lax.axis_index("sp") // CORES
        copies = []
        for slot in reversed(range(chips)):
            targets = (kv_refs[slot].at[0], kv_refs[slot].at[1], q_refs[slot])
            for part, source in enumerate((k_ref, v_ref, q_ref)):
                flip = flip_of((q_slots if part == 2 else kv_slots)[slot])
                columns = pl.ds(pl.multiple_of((chip ^ flip) * width, HD), width)
                copies.append(
                    pltpu.make_async_copy(
                        source.at[0, :, columns], targets[part], sems.at[3 * slot + part]
                    )
                )
        for copy in copies:
            copy.start()
        for copy in copies:
            copy.wait()

    outs = pl.pallas_call(
        body,
        out_shape=[pltpu.VMEM((2, rows, width), keys.dtype)] * chips
        + [pltpu.VMEM((rows, width), values.dtype)] * chips,
        in_specs=[ANY] * 3,
        out_specs=in_vmem(2 * chips),
        scratch_shapes=[pltpu.SemaphoreType.DMA((3 * chips,))],
        name="pack",
    )(queries, keys, values)
    return outs[:chips], outs[chips:]


def join(blocks, slots, flops=0):
    chips, parts = len(blocks), blocks[0].shape[:-2]
    rows, width = blocks[0].shape[-2:]
    count = parts[0] if parts else 1

    def body(*refs):
        for slot, block in enumerate(refs[:chips]):
            for part, out in enumerate(refs[chips:]):
                out[chip_rows(flip_of(slots[(slot + 1) % chips]), rows), :] = block[part] if parts else block[...]

    return pl.pallas_call(
        body,
        out_shape=[pltpu.VMEM((chips * rows, width), blocks[0].dtype)] * count,
        in_specs=in_vmem(chips),
        out_specs=in_vmem(count),
        cost_estimate=pl.CostEstimate(flops=flops, bytes_accessed=0, transcendentals=0),
        name="join",
    )(*resident(*blocks[1:], blocks[0]))


def hold(blocks, after=(), flops=0):
    count = len(blocks)

    def body(*refs):
        for source, target in zip(refs[:count], refs[count + len(after) : -1]):
            target[...] = source[...]
        refs[-1][...] = jnp.zeros_like(refs[-1])

    return pl.pallas_call(
        body,
        out_shape=[pltpu.VMEM(block.shape, block.dtype) for block in blocks] + [pltpu.VMEM((8, HD), jnp.float32)],
        in_specs=in_vmem(count + len(after)),
        out_specs=in_vmem(count + 1),
        cost_estimate=pl.CostEstimate(flops=flops, bytes_accessed=0, transcendentals=0),
        name="hold",
    )(*resident(*blocks, *after))


def pair(first, second):
    def body(first_ref, second_ref, out_ref):
        out_ref[0] = first_ref[...]
        out_ref[1] = second_ref[...]

    return pl.pallas_call(
        body,
        out_shape=pltpu.VMEM((2, *first.shape), first.dtype),
        in_specs=in_vmem(2),
        out_specs=in_vmem(1)[0],
        name="pair",
    )(*resident(first, second))


def chip_rows(flip, rows):
    chip = lax.axis_index("sp") // CORES
    return pl.ds(pl.multiple_of((chip ^ flip) * rows, rows), rows)


def turn(x, bit):
    return lax.ppermute(x, "grp", [(i, i ^ (1 << bit)) for i in range(lax.axis_size("grp"))])


def choose(mine, theirs, anchor, bit, after=()):
    def body(anchor_ref, mine_ref, theirs_ref, *rest):
        out_ref = rest[-1]
        same = ((anchor_ref[0] % lax.axis_size("grp") ^ lax.axis_index("grp")) >> bit) & 1

        @pl.when(same == 0)
        def _():
            out_ref[...] = mine_ref[...]

        @pl.when(same != 0)
        def _():
            out_ref[...] = theirs_ref[...]

    return pl.pallas_call(
        body,
        out_shape=pltpu.VMEM(mine.shape, mine.dtype),
        in_specs=[SMEM] + in_vmem(2 + len(after)),
        out_specs=in_vmem(1)[0],
        name="choose",
    )(anchor, *resident(mine, theirs, *after))


def scores_of(q, k_ref, columns):
    return lax.dot_general(
        q, k_ref[:, columns], (((1,), (1,)), ((), ())), preferred_element_type=jnp.float32
    )


def mix(weights, v_ref, columns):
    return jnp.dot(weights, v_ref[:, columns], preferred_element_type=jnp.float32)


def each_chunk(length, chunk):
    step = min(256, length)
    if length == step:
        chunk(0, step)
    else:
        pl.loop(0, length // step)(lambda index: chunk(pl.multiple_of(index * step, step), step))


def cost(length, width):
    return pl.CostEstimate(
        flops=8 * length * length * width,
        bytes_accessed=0,
        transcendentals=2 * length * length * (width // HD),
    )


def weigh(q, own_k, other_k, columns, own_mask, other_mask, before=None):
    first = own_mask(scores_of(q, own_k, columns))
    second = other_mask(scores_of(q, other_k, columns))
    top = jnp.maximum(jnp.max(first, axis=1, keepdims=True), jnp.max(second, axis=1, keepdims=True))
    if before is not None:
        top = jnp.maximum(top, before)
    first = jnp.exp2((first - top) * EXP_SCALE)
    second = jnp.exp2((second - top) * EXP_SCALE)
    total = jnp.sum(first, axis=1, keepdims=True) + jnp.sum(second, axis=1, keepdims=True)
    return first.astype(jnp.bfloat16), second.astype(jnp.bfloat16), top, total


def near(q_rows, own_k, own_v, other, positions):
    length, width = q_rows.shape
    chips = lax.axis_size("sp") // CORES
    rows = length // chips
    paired = CORES * rows == HD and chips % 2 == 0
    if not paired:
        positions = jnp.swapaxes(positions.reshape(chips, CORES, rows), 0, 1).reshape(CORES, length)

    def split(at):
        if not paired:
            return [jnp.broadcast_to(at[c : c + 1, :], (8, length)) for c in range(CORES)]
        low = lax.broadcasted_iota(jnp.int32, (8, HD), 1) < rows
        tokens = [jnp.broadcast_to(at[:, c * HD : (c + 1) * HD], (8, HD)) for c in range(chips)]
        turned = [pltpu.roll(row, rows, 1) for row in tokens]
        pairs = range(0, chips, 2)
        return [
            jnp.concatenate([jnp.where(low, tokens[c], turned[c + 1]) for c in pairs], 1),
            jnp.concatenate([jnp.where(low, turned[c], tokens[c + 1]) for c in pairs], 1),
        ]

    def body(q_ref, own_k, own_v, other_kv, at, top_ref, sum_ref, acc_ref, end_ref, own_at):
        end_ref[...] = jnp.zeros_like(end_ref)
        other_k, other_v = other_kv.at[0], other_kv.at[1]
        core = lax.axis_index("sp") % CORES
        first_at, second_at = split(at)
        own_at[...] = jnp.where(core == 0, first_at, second_at)
        other_at = jnp.where(core == 0, second_at, first_at)[:1, :]

        def chunk(start, step):
            here = pl.ds(start, step)
            order = jnp.transpose(jnp.broadcast_to(own_at[:1, here], (HD, step)))[:, :1]
            for head in range(width // HD):
                columns = slice(head * HD, (head + 1) * HD)
                first, second, top, total = weigh(
                    q_ref[here, columns],
                    own_k,
                    other_k,
                    columns,
                    lambda scores: jnp.where(own_at[:1, :] <= order, scores, NEG),
                    lambda scores: jnp.where(other_at <= order, scores, NEG),
                )
                top_ref[head, here, :] = jnp.broadcast_to(top, (step, HD))
                sum_ref[head, here, :] = jnp.broadcast_to(total, (step, HD))
                acc_ref[here, columns] = mix(first, own_v, columns) + mix(second, other_v, columns)

        each_chunk(length, chunk)

    state = pltpu.VMEM((width // HD, length, HD), jnp.float32)
    return pl.pallas_call(
        body,
        out_shape=[
            state,
            state,
            pltpu.VMEM((length, width), jnp.float32),
            pltpu.VMEM((8, HD), jnp.float32),
        ],
        in_specs=in_vmem(5),
        out_specs=in_vmem(4),
        scratch_shapes=[pltpu.VMEM((8, length), jnp.int32)],
        compiler_params=pltpu.CompilerParams(vmem_limit_bytes=VMEM_LIMIT),
        cost_estimate=cost(length, width),
        name="near",
    )(*resident(q_rows, own_k, own_v, other), positions)


def far_weights(q_rows, top, own_k, other_k, anchor):
    length, width = q_rows.shape
    heads = width // HD

    def body(anchor_ref, q_ref, old_ref, own_k, other_k, first_ref, second_ref, top_ref, sum_ref):
        hidden = lax.axis_index("grp") == anchor_ref[0] % lax.axis_size("grp")

        def mask(scores):
            return jnp.where(hidden, NEG, scores)

        def chunk(start, step):
            here = pl.ds(start, step)
            for head in range(heads):
                columns = slice(head * HD, (head + 1) * HD)
                old = old_ref[head, here, :][:, :1]
                first, second, top, total = weigh(
                    q_ref[here, columns], own_k, other_k, columns, mask, mask, old
                )
                first_ref[head, here, :] = first
                second_ref[head, here, :] = second
                top_ref[head, here, :] = jnp.broadcast_to(top, (step, HD))
                sum_ref[head, here, :] = jnp.broadcast_to(total, (step, HD))

        each_chunk(length, chunk)

    weights = pltpu.VMEM((heads, length, length), jnp.bfloat16)
    state = pltpu.VMEM((heads, length, HD), jnp.float32)
    return pl.pallas_call(
        body,
        out_shape=[weights, weights, state, state],
        in_specs=[SMEM] + in_vmem(4),
        out_specs=in_vmem(4),
        compiler_params=pltpu.CompilerParams(vmem_limit_bytes=VMEM_LIMIT),
        cost_estimate=cost(length, width),
        name="far_weights",
    )(anchor, *resident(q_rows, top, own_k, other_k))


def far_values(near_state, far_state, own_v, other_v, slots):
    length, width = near_state[-1].shape
    chips = lax.axis_size("sp") // CORES
    rows = length // chips

    def body(*refs):
        old_top, old_sum, old_acc, first_ref, second_ref, top_ref, sum_ref, own_v, other_v = refs[:9]
        out_refs, done = refs[9:-1], refs[-1]

        def chunk(start, step):
            here = pl.ds(start, step)
            for head in range(width // HD):
                columns = slice(head * HD, (head + 1) * HD)
                keep = jnp.exp2((old_top[head, here, :] - top_ref[head, here, :]) * EXP_SCALE)
                total = keep * old_sum[head, here, :] + sum_ref[head, here, :]
                acc = (
                    keep * old_acc[here, columns]
                    + mix(first_ref[head, here, :], own_v, columns)
                    + mix(second_ref[head, here, :], other_v, columns)
                )
                done[here, columns] = (acc / total).astype(jnp.bfloat16)

        each_chunk(length, chunk)
        for slot, out in enumerate(out_refs):
            out[...] = done[chip_rows(flip_of(slots[slot]), rows), :]

    return pl.pallas_call(
        body,
        out_shape=[pltpu.VMEM((rows, width), jnp.bfloat16)] * chips,
        in_specs=in_vmem(9),
        out_specs=in_vmem(chips),
        scratch_shapes=[pltpu.VMEM((length, width), jnp.bfloat16)],
        compiler_params=pltpu.CompilerParams(vmem_limit_bytes=VMEM_LIMIT),
        cost_estimate=cost(length, width),
        name="far_values",
    )(*resident(*near_state, *far_state, own_v, other_v))


def unpack(blocks, slots):
    chips = len(blocks)
    rows, width = blocks[0].shape

    def body(*refs):
        block_refs, out_ref, sems = refs[:chips], refs[chips], refs[-1]
        chip = lax.axis_index("sp") // CORES
        copies = []
        for slot, block in enumerate(block_refs):
            flip = flip_of(slots[(slot + 1) % chips])
            columns = pl.ds(pl.multiple_of((chip ^ flip) * width, HD), width)
            copies.append(pltpu.make_async_copy(block, out_ref.at[0, :, columns], sems.at[slot]))
        for copy in copies:
            copy.start()
        for copy in copies:
            copy.wait()

    return pl.pallas_call(
        body,
        out_shape=jax.ShapeDtypeStruct((1, rows, chips * width), blocks[0].dtype),
        in_specs=in_vmem(chips),
        out_specs=ANY,
        scratch_shapes=[pltpu.SemaphoreType.DMA((chips,))],
        name="unpack",
    )(*resident(*blocks[1:], blocks[0]))


def trade(blocks, slots):
    devices = lax.axis_size("sp")
    moved = [
        lax.ppermute(block, "sp", [(i, i ^ (CORES * flips[i % CORES])) for i in range(devices)])
        for block, flips in zip(blocks[1:], slots[1:])
    ]
    return [blocks[0], *moved]


def on_device(queries, keys, values, positions, anchor):
    chips = lax.axis_size("sp") // CORES
    distant_first = [*reversed(range(1, chips))]
    crossing_first = sorted(distant_first, key=lambda flip: (flip < chips // 2, flip))
    kv_slots = [(0, 0), *zip(crossing_first, crossing_first)]
    q_slots = [(0, 0), *zip(crossing_first, crossing_first)]
    out_slots = [(0, 0), *zip(distant_first, distant_first)]

    kv_blocks, q_blocks = pack(queries, keys, values, kv_slots, q_slots)
    moved = trade([q_blocks[0], q_blocks[-1]], [q_slots[0], q_slots[-1]])
    nearest, _ = hold(moved[1:], flops=QUERY_FLOPS)
    moved = [moved[0], nearest]
    k_own, v_own = join(trade(kv_blocks, kv_slots), kv_slots)
    other = swap(pair(k_own, v_own), 1)
    *distant, seen = hold(trade(q_blocks[:-1], q_slots[:-1])[1:], flops=QUERY_FLOPS)
    (q_rows,) = join([*moved[:1], *distant, *moved[1:]], q_slots)

    bits = lax.axis_size("grp").bit_length() - 1
    k_far, v_far, *state, end = k_own, v_own, *near(q_rows, k_own, v_own, other, positions)
    for stage in range(bits):
        after = [[seen], [end]][stage] if stage < 2 else ()
        back = bits - 1 - stage
        k_far = choose(k_far, turn(k_far, stage), anchor, stage, after)
        v_far = choose(v_far, turn(v_far, back), anchor, back)
    far_state = far_weights(q_rows, state[0], k_far, swap(k_far, 1), anchor)
    done = far_values(state, far_state, v_far, swap(v_far, 1), out_slots)
    return unpack(trade(done, out_slots), out_slots)


def solution(mesh):
    return jax.shard_map(
        on_device,
        mesh=mesh,
        in_specs=(
            P("grp", "sp", None),
            P("grp", "sp", None),
            P("grp", "sp", None),
            P("grp", None),
            P(),
        ),
        out_specs=P("grp", "sp", None),
        check_vma=False,
    )
```
